128 devices in a mesh: lead: 4 (over x_lo, core), space: 32 (over z, y, x_hi).
Axes of the slice: x: 4 (x_hi: 2, x_lo: 2; x = x_hi * 2 + x_lo), y: 4, z: 4, core: 2. Of those that a mesh axis runs over, the one named last changes fastest.
Arguments:
- latent: bfloat16 [4, 128, 256, 512], P('lead', 'space'), may hold values from -6 to 6
- lead_index: int32 [4], P('lead'), may hold values from 0 to 720
- conv_kernel: float32 [3, 3, 512], replicated, may hold values from -2.5 to 2.5
- cond_table: float32 [721, 2, 512], replicated, may hold values from -3 to 3
- w_qkv: bfloat16 [512, 1536], replicated, may hold values from -0.25 to 0.25
- w_out: bfloat16 [512, 512], replicated, may hold values from -0.25 to 0.25
- cotangent: bfloat16 [4, 128, 256, 512], P('lead', 'space'), may hold values from -6 to 6
Outputs:
- grad_x: bfloat16 [4, 128, 256, 512], P('lead', 'space')
- grad_qkv: float32 [512, 1536], replicated
- grad_out: float32 [512, 512], replicated
- grad_kernel: float32 [3, 3, 512], replicated
- grad_table: float32 [721, 2, 512], replicated
The draws below stay inside these ranges and needn't reach their ends.
All inputs are finite; a program needn't handle non-finite values.
Results may differ from the reference program's by a relative error of at most 0.0095.
Values may be sent and summed in bfloat16 or wider, within the bound.
A program may use at most 128 MiB of HBM per device.

```python
import math
import jax
import jax.numpy as jnp
from jax import lax

D = 512
HEADS = 16
HDIM = 32
GRID = 8
LEADS = 721
L = 4
H = 128
W = 256


def touch_ends(drawn, key, least, high):
    place = [jax.random.randint(jax.random.fold_in(key, axis), (), 0, length) for axis, length in enumerate(drawn.shape)]
    longest = drawn.shape.index(max(drawn.shape))
    beside = place[:longest] + [(place[longest] + 1) % drawn.shape[longest]] + place[longest + 1:]
    return drawn.at[tuple(place)].set(least).at[tuple(beside)].set(high)


def levels(own_key, extent, pieces, smallest, largest):
    gain = 1.0
    for position, shards_of in pieces:
        draws = jax.random.uniform(jax.random.fold_in(jax.random.fold_in(own_key, 6), position), (shards_of,), jnp.float32, smallest / len(pieces), largest / len(pieces))
        gain = gain * jnp.repeat(jnp.exp(draws), extent[position] // shards_of).reshape((-1,) + (1,) * (len(extent) - 1 - position))
    return gain


def gaussian(own_key, dims, scale, bound, cuts=(), held_as=jnp.bfloat16):
    gain = levels(own_key, dims, cuts, -0.22, 0.18) if cuts else 1.0
    entries = jax.random.normal(own_key, dims, jnp.float32) * scale * gain
    return jnp.minimum(jnp.maximum(entries, -bound), bound).astype(held_as)


def setup_inputs(seed: int = 0) -> dict:
    key_list = jax.random.split(jax.random.key(seed), 8)
    latent = gaussian(key_list[0], (L, H, W, D), 1.0, 6.0, ((0, 4), (1, 32)))
    lead_index = touch_ends(jax.random.randint(key_list[1], (L,), 0, LEADS), jax.random.fold_in(key_list[1], 1), 0, LEADS - 1).astype(jnp.int32)
    conv_kernel = gaussian(key_list[2], (3, 3, D), 0.3, 2.5, (), jnp.float32)
    cond_table = gaussian(key_list[3], (LEADS, 2, D), 0.5, 3.0, (), jnp.float32)
    w_qkv = gaussian(key_list[4], (D, 3 * D), D ** -0.5, 0.25)
    w_out = gaussian(key_list[5], (D, D), D ** -0.5, 0.25)
    cotangent = gaussian(key_list[6], (L, H, W, D), 1.0, 6.0, ((0, 4), (1, 32)))
    return dict(latent=latent, lead_index=lead_index, conv_kernel=conv_kernel, cond_table=cond_table, w_qkv=w_qkv, w_out=w_out, cotangent=cotangent)


EPSILON = 1e-05

def to_groups(tensor):
    shape = tensor.shape
    blocks = tensor.reshape(GRID, shape[0] // GRID, GRID, shape[1] // GRID, shape[2])
    blocks = blocks.transpose(1, 3, 0, 2, 4)
    return blocks.reshape(-1, GRID * GRID, shape[2])

def from_groups(groups, height, breadth):
    channels = groups.shape[-1]
    blocks = groups.reshape(height // GRID, breadth // GRID, GRID, GRID, channels)
    blocks = blocks.transpose(2, 0, 3, 1, 4)
    return blocks.reshape(height, breadth, channels)

def split_heads(tensor):
    shape = tensor.shape
    return tensor.reshape(shape[0], shape[1], HEADS, HDIM).astype(jnp.float32)

def widen(tensor):
    return lax.optimization_barrier(tensor.astype(jnp.bfloat16)).astype(jnp.float32)

def one_sample(tensor, lead_time, cotan, conv_kernel, cond_table, w_qkv, w_out):
    height, breadth, channels = tensor.shape
    score_scale = 1.0 / math.sqrt(HDIM)
    padded = jnp.pad(tensor, ((1, 1), (1, 1), (0, 0))).astype(jnp.float32)
    smoothed = jnp.zeros((height, breadth, channels), jnp.float32)
    for offset_row in range(3):
        for offset_col in range(3):
            smoothed = smoothed + conv_kernel[offset_row, offset_col] * padded[offset_row:offset_row + height, offset_col:offset_col + breadth]
    residual = tensor.astype(jnp.float32) + smoothed
    centred = residual - lax.optimization_barrier(jnp.mean(residual, axis=-1, keepdims=True))
    inverse = lax.rsqrt(lax.optimization_barrier(jnp.mean(centred * centred, axis=-1, keepdims=True)) + EPSILON)
    normal_form = centred * inverse
    onehot = (jnp.arange(LEADS, dtype=jnp.int32) == lead_time).astype(jnp.float32)
    modulation = jnp.dot(onehot[None, :], cond_table.reshape(LEADS, 2 * channels), precision=lax.Precision.HIGHEST).reshape(2, channels)
    normed = (normal_form * (1.0 + modulation[0]) + modulation[1]).astype(jnp.bfloat16)
    flat_normed = normed.reshape(-1, channels)
    projected = jnp.dot(flat_normed, w_qkv, preferred_element_type=jnp.float32).astype(jnp.bfloat16)
    groups = to_groups(projected.reshape(height, breadth, 3 * channels))
    queries = split_heads(groups[..., :channels])
    keys_all = split_heads(groups[..., channels:2 * channels])
    values = split_heads(groups[..., 2 * channels:])
    scores = jnp.einsum('gqhe,gkhe->ghqk', queries, keys_all) * score_scale
    probabilities = jax.nn.softmax(scores, axis=-1)
    weights = widen(probabilities)
    attended = jnp.einsum('ghqk,gkhe->gqhe', weights, values).astype(jnp.bfloat16)
    cot_groups = to_groups(cotan).reshape(-1, channels)
    grad_out = jnp.dot(attended.reshape(-1, channels).T, cot_groups, preferred_element_type=jnp.float32)
    d_att = jnp.dot(cot_groups, w_out.T, preferred_element_type=jnp.float32).astype(jnp.bfloat16)
    d_heads = split_heads(d_att.reshape(groups.shape[0], GRID * GRID, channels))
    d_probs = jnp.einsum('gqhe,gkhe->ghqk', d_heads, values)
    d_scores = widen(probabilities * (d_probs - lax.optimization_barrier(jnp.sum(probabilities * d_probs, axis=-1, keepdims=True))))
    d_query = jnp.einsum('ghqk,gkhe->gqhe', d_scores, keys_all) * score_scale
    d_key = jnp.einsum('ghqk,gqhe->gkhe', d_scores, queries) * score_scale
    d_value = jnp.einsum('ghqk,gqhe->gkhe', weights, d_heads)
    group_shape = (groups.shape[0], GRID * GRID, channels)
    d_groups = jnp.concatenate([d_query.reshape(group_shape), d_key.reshape(group_shape), d_value.reshape(group_shape)], axis=-1).astype(jnp.bfloat16)
    d_projected = from_groups(d_groups, height, breadth).reshape(-1, 3 * channels)
    grad_qkv = jnp.dot(flat_normed.T, d_projected, preferred_element_type=jnp.float32)
    d_normed = jnp.dot(d_projected, w_qkv.T, preferred_element_type=jnp.float32).astype(jnp.bfloat16)
    d_normed = d_normed.astype(jnp.float32).reshape(height, breadth, channels)
    table_rows = jnp.stack([lax.optimization_barrier(jnp.sum(d_normed * normal_form, axis=(0, 1))), lax.optimization_barrier(jnp.sum(d_normed, axis=(0, 1)))])
    gradient = d_normed * (1.0 + modulation[0])
    d_residual = cotan.astype(jnp.float32) + inverse * (gradient - lax.optimization_barrier(jnp.mean(gradient, axis=-1, keepdims=True)) - normal_form * lax.optimization_barrier(jnp.mean(gradient * normal_form, axis=-1, keepdims=True)))
    padded_d = jnp.pad(d_residual, ((1, 1), (1, 1), (0, 0)))
    grad_kernel = []
    grad_field = d_residual
    for offset_row in range(3):
        for offset_col in range(3):
            grad_kernel.append(lax.optimization_barrier(jnp.sum(d_residual * padded[offset_row:offset_row + height, offset_col:offset_col + breadth], axis=(0, 1))))
            grad_field = grad_field + conv_kernel[offset_row, offset_col] * padded_d[2 - offset_row:2 - offset_row + height, 2 - offset_col:2 - offset_col + breadth]
    grad_kernel = jnp.stack(grad_kernel).reshape(3, 3, channels)
    return (grad_field.astype(jnp.bfloat16), grad_qkv, grad_out, grad_kernel, table_rows)

def reference(latent, lead_index, conv_kernel, cond_table, w_qkv, w_out, cotangent):
    channels = latent.shape[-1]

    def apply(items):
        return one_sample(items[0], items[1], items[2], conv_kernel, cond_table, w_qkv, w_out)
    grad_x, grad_qkv, grad_out, grad_kernel, table_rows = lax.map(apply, (latent, lead_index, cotangent))
    norm_scale = 1.0 / math.sqrt(L * H * W)
    onehot = (lead_index[:, None] == jnp.arange(LEADS, dtype=jnp.int32)[None, :]).astype(jnp.float32)
    grad_table = jnp.dot(onehot.T, table_rows.reshape(-1, 2 * channels), precision=lax.Precision.HIGHEST).reshape(LEADS, 2, channels)
    return (grad_x, lax.optimization_barrier(jnp.sum(grad_qkv, axis=0)) * norm_scale, lax.optimization_barrier(jnp.sum(grad_out, axis=0)) * norm_scale, lax.optimization_barrier(jnp.sum(grad_kernel, axis=0)) * norm_scale, grad_table * norm_scale)
```

```python
import functools
import math

import jax
import jax.numpy as jnp
from jax import lax
from jax.experimental import pallas as pl
from jax.experimental.pallas import tpu as pltpu
from jax.sharding import PartitionSpec as P

HDIM = 32
GRID = 8
EPSILON = 1e-05
ROWS = 4
COLS = 256
D = 512
PEERS = 8
CHUNK = 32
MESH = pl.DeviceIdType.MESH
F32 = jnp.float32
BF16 = jnp.bfloat16
VMEM_LIMIT = 52 * 1024 * 1024


def remote(src, dst, send, recv, device):
    return pltpu.make_async_remote_copy(
        src_ref=src, dst_ref=dst, send_sem=send, recv_sem=recv, device_id=device, device_id_type=MESH
    )


def dot(a, b, ca, cb):
    return lax.dot_general(a, b, (((ca,), (cb,)), ((), ())), preferred_element_type=F32)


def place():
    lead = lax.axis_index("lead")
    space = lax.axis_index("space")
    return lead, space


def send_order():
    p = lax.broadcasted_iota(jnp.int32, (COLS, COLS), 0)
    col = lax.broadcasted_iota(jnp.int32, (COLS, COLS), 1)
    return jnp.where((p & 7) * 32 + (p >> 5) * 4 + ((p >> 3) & 3) == col, 1.0, 0.0).astype(BF16)


def field_order():
    p = lax.broadcasted_iota(jnp.int32, (COLS, COLS), 1)
    col = lax.broadcasted_iota(jnp.int32, (COLS, COLS), 0)
    return jnp.where((p & 7) * 32 + (p >> 5) * 4 + ((p >> 3) & 3) == col, 1.0, 0.0).astype(BF16)


def group_order():
    g = lax.broadcasted_iota(jnp.int32, (COLS, COLS), 0)
    p = lax.broadcasted_iota(jnp.int32, (COLS, COLS), 1)
    return jnp.where(((g >> 3) & 7) * 32 + (g >> 6) * 8 + (g & 7) == p, 1.0, 0.0).astype(BF16)


def forward_kernel(
    latent, cot, ck, mod, xg, cg, nf, inv, halo, xp, xs, cs, nrm, perm, hsem, xsem, csem, lsem
):
    lead, space = place()
    a, q = space // 4, lax.rem(space, 4)

    def peer(d):
        return lax.rem(a + d, PEERS)

    @pl.when(space == 0)
    def _():
        halo[0] = jnp.zeros((COLS, D), BF16)

    @pl.when(space == 31)
    def _():
        halo[1] = jnp.zeros((COLS, D), BF16)

    barrier = pltpu.get_barrier_semaphore()

    def greet(d, c):
        pl.semaphore_signal(barrier, inc=1, device_id=(lead, 4 * peer(d) + q), device_id_type=MESH)
        return c

    lax.fori_loop(1, PEERS, greet, 0)

    @pl.when(space > 0)
    def _():
        pl.semaphore_signal(barrier, inc=1, device_id=(lead, space - 1), device_id_type=MESH)

    @pl.when(space < 31)
    def _():
        pl.semaphore_signal(barrier, inc=1, device_id=(lead, space + 1), device_id_type=MESH)

    low = jnp.where(space > 0, 1, 0)
    high = jnp.where(space < 31, 1, 0)
    perm[...] = send_order()
    pl.semaphore_wait(barrier, 7 + low + high)

    def up():
        return remote(latent.at[0], halo.at[1], hsem.at[0], hsem.at[2], (lead, space - 1))

    def down():
        return remote(latent.at[3], halo.at[0], hsem.at[1], hsem.at[3], (lead, space + 1))

    @pl.when(space > 0)
    def _():
        up().start()

    @pl.when(space < 31)
    def _():
        down().start()

    def send(bufs, out, sem, r):
        def one(d, c):
            t = peer(d)
            remote(bufs.at[r, t], out.at[r, a], sem.at[0, r, d], sem.at[1, r, d], (lead, 4 * t + q)).start()
            return c

        lax.fori_loop(1, PEERS, one, 0)
        pltpu.make_async_copy(bufs.at[r, a], out.at[r, a], sem.at[0, r, 0]).start()

    def finish(bufs, out, sem, r):
        def one(d, c):
            t = peer(d)
            f = lax.rem(a + PEERS - d, PEERS)
            remote(bufs.at[r, t], out.at[r, f], sem.at[0, r, d], sem.at[1, r, d], (lead, 4 * t + q)).wait()
            return c

        lax.fori_loop(1, PEERS, one, 0)
        pltpu.make_async_copy(bufs.at[r, a], out.at[r, a], sem.at[0, r, 0]).wait()

    def cot_row(r, c):
        cs[r] = dot(perm[...], cot[r], 1, 0).astype(BF16).reshape(PEERS, CHUNK, D)
        send(cs, cg, csem, r)
        return c

    cot_row(1, 0)
    cot_row(2, 0)

    xp[:, 0:8, :] = jnp.zeros((ROWS + 2, 8, D), F32)
    xp[:, COLS + 8 : COLS + 16, :] = jnp.zeros((ROWS + 2, 8, D), F32)

    def widen(r, c):
        xp[r + 1, 8 : COLS + 8, :] = latent[r].astype(F32)
        return c

    lax.fori_loop(0, ROWS, widen, 0)

    def row(r):
        def chunk(c, carry):
            at = pl.multiple_of(c * CHUNK, CHUNK)
            w = [xp[r + m, pl.ds(at, CHUNK + 16), :] for m in range(3)]
            k = [ck[m : m + 1, :] for m in range(9)]
            t = [k[j] * w[0] + k[3 + j] * w[1] + k[6 + j] * w[2] for j in range(3)]
            res = w[1][8 : CHUNK + 8] + (
                t[0][7 : CHUNK + 7] + t[1][8 : CHUNK + 8] + t[2][9 : CHUNK + 9]
            )
            cen = res - jnp.mean(res, axis=-1, keepdims=True)
            iv = lax.rsqrt(jnp.mean(cen * cen, axis=-1, keepdims=True) + EPSILON)
            n = cen * iv
            nf[r, pl.ds(at, CHUNK), :] = n
            inv[r, pl.ds(at, CHUNK), :] = jnp.broadcast_to(iv, (CHUNK, 128))
            nrm[pl.ds(at, CHUNK), :] = (n * (1.0 + mod[0:1, :]) + mod[1:2, :]).astype(BF16)
            return carry

        lax.fori_loop(0, COLS // CHUNK, chunk, 0)
        xs[r] = dot(perm[...], nrm[...], 1, 0).astype(BF16).reshape(PEERS, CHUNK, D)
        send(xs, xg, xsem, r)

    row(1)
    row(2)
    cot_row(0, 0)
    cot_row(3, 0)

    @pl.when(space > 0)
    def _():
        up().wait_send()
        remote(latent.at[3], halo.at[0], hsem.at[1], hsem.at[3], (lead, space - 1)).wait_recv()

    @pl.when(space < 31)
    def _():
        down().wait_send()
        remote(latent.at[0], halo.at[1], hsem.at[0], hsem.at[2], (lead, space + 1)).wait_recv()

    xp[0, 8 : COLS + 8, :] = halo[0].astype(F32)
    xp[ROWS + 1, 8 : COLS + 8, :] = halo[1].astype(F32)
    row(0)
    row(3)
    for r in (1, 2, 0, 3):
        finish(cs, cg, csem, r)
        finish(xs, xg, xsem, r)


def attention_row(x, c, wqkv, wout, xg, cg, qkv, da, att, dp, dn, perm, i):
    scale = 1.0 / math.sqrt(HDIM)
    base = pl.multiple_of(i * COLS, COLS)
    here = pl.ds(base, COLS)
    gx = dot(perm[...], x, 1, 0).astype(BF16)
    gc = dot(perm[...], c, 1, 0).astype(BF16)
    xg[here, :] = gx
    cg[here, :] = gc
    for n in range(3):
        qkv[:, n * D : (n + 1) * D] = dot(gx, wqkv[:, n * D : (n + 1) * D], 1, 0).astype(BF16)
    da[...] = dot(gc, wout[...], 1, 1).astype(BF16)
    lane = lax.broadcasted_iota(jnp.int32, (1, 128), 1) // HDIM
    masks = [jnp.where(lane == h, 1.0, 0.0) for h in range(4)]
    masks16 = [m.astype(BF16) for m in masks]

    def spread(t):
        return jnp.concatenate([t * m for m in masks16], axis=0)

    def gather(t):
        total = t[0:64] * masks[0]
        for h in range(1, 4):
            total = total + t[64 * h : 64 * h + 64] * masks[h]
        return total

    def group(g, carry):
        rows = pl.ds(pl.multiple_of(g * 64, 64), 64)
        out = pl.ds(pl.multiple_of(base + g * 64, 64), 64)
        for t in range(4):
            lo, hi = t * 128, t * 128 + 128
            qs = spread(qkv[rows, lo:hi])
            k = qkv[rows, D + lo : D + hi]
            v = qkv[rows, 2 * D + lo : 2 * D + hi]
            ds_ = spread(da[rows, lo:hi])
            s = dot(k, qs, 1, 1) * scale
            e = jnp.exp(s - jnp.max(s, axis=0, keepdims=True))
            p = e * (1.0 / jnp.sum(e, axis=0, keepdims=True))
            p16 = p.astype(BF16)
            att[out, lo:hi] = gather(dot(p16, v, 0, 0)).astype(BF16)
            dpr = dot(v, ds_, 1, 1)
            inner = jnp.sum(p * dpr, axis=0, keepdims=True)
            dsc = (p * (dpr - inner)).astype(BF16)
            dp[out, lo:hi] = (gather(dot(dsc, k, 0, 0)) * scale).astype(BF16)
            dp[out, D + lo : D + hi] = (dot(dsc, qs, 1, 0) * scale).astype(BF16)
            dp[out, 2 * D + lo : 2 * D + hi] = dot(p16, ds_, 1, 0).astype(BF16)
        return carry

    lax.fori_loop(0, 4, group, 0)
    dnf = dot(dp[here, :], wqkv[...], 1, 1).astype(BF16).astype(F32)
    blocks = [dnf[g * 64 + m * 8 : g * 64 + m * 8 + 8] for m in range(8) for g in range(4)]
    dn[i] = jnp.concatenate(blocks, axis=0).astype(BF16).reshape(PEERS, CHUNK, D)


def attention_kernel(x, c, wqkv, wout, dn, grads, xg, cg, qkv, da, att, dp, perm):
    perm[...] = group_order()

    def row(i, carry):
        attention_row(
            x[i].reshape(COLS, D), c[i].reshape(COLS, D), wqkv, wout, xg, cg, qkv, da, att, dp, dn, perm, i
        )
        return carry

    lax.fori_loop(0, ROWS, row, 0)
    for h in range(2):
        for n in range(4):
            if n < 3:
                g = dot(xg[:, h * 256 : h * 256 + 256], dp[:, n * D : (n + 1) * D], 0, 0)
            else:
                g = dot(att[:, h * 256 : h * 256 + 256], cg[...], 0, 0)
            grads[h, n] = g.astype(BF16)


def backward_kernel(
    dn, grads, nf, inv, mod, cot, latent, halo, ck, leadrow,
    gx, total, small,
    dr, dnf, xp, dpad, hsend, hrecv, perm, r0, r1, r2, r3, a0, a1, a2, a3, ksum, tsum, sm, s1, s2, s3, s4,
    dsem, hsem, rsem, gsem, ssem,
):
    lead, space = place()
    a, q = space // 4, lax.rem(space, 4)
    core, x_lo = lax.rem(lead, 2), lead // 2
    z, y, x_hi = space // 8, lax.rem(space // 2, 4), lax.rem(space, 2)
    x = x_hi * 2 + x_lo
    coord = {"x": x, "y": y, "z": z}

    def at_axis(axis, j):
        if axis == "x":
            return ((lax.rem(j, 2) * 2 + core), space - x_hi + j // 2)
        if axis == "y":
            return (lead, space + (j - y) * 2)
        return (lead, space + (j - z) * 8)

    def ahead(axis, d):
        return lax.rem(coord[axis] + d, 4)

    def behind(axis, d):
        return lax.rem(coord[axis] + 4 - d, 4)

    twin = (lead + 1 - 2 * core, space)

    @pl.when(space == 0)
    def _():
        hrecv[0] = jnp.zeros((COLS, D), BF16)

    @pl.when(space == 31)
    def _():
        hrecv[1] = jnp.zeros((COLS, D), BF16)

    barrier = pltpu.get_barrier_semaphore()

    def greet(device):
        pl.semaphore_signal(barrier, inc=1, device_id=device, device_id_type=MESH)

    def greet_peer(d, c):
        greet((lead, 4 * lax.rem(a + d, PEERS) + q))
        return c

    lax.fori_loop(1, PEERS, greet_peer, 0)
    for axis in "xyz":
        for d in range(1, 4):
            greet(at_axis(axis, ahead(axis, d)))
    greet(twin)

    @pl.when(space > 0)
    def _():
        greet((lead, space - 1))

    @pl.when(space < 31)
    def _():
        greet((lead, space + 1))

    perm[...] = field_order()
    pl.semaphore_wait(barrier, 17 + jnp.where(space > 0, 1, 0) + jnp.where(space < 31, 1, 0))

    def swap():
        return remote(grads.at[1 - core], r0, rsem.at[0], rsem.at[1], twin)

    swap().start()

    def dn_copy(r, d):
        t = lax.rem(a + d, PEERS)
        return remote(dn.at[r, t], dr.at[r, a], dsem.at[0, r, d], dsem.at[1, r, d], (lead, 4 * t + q))

    def dn_send(r, c):
        def one(d, c):
            dn_copy(r, d).start()
            return c

        lax.fori_loop(1, PEERS, one, 0)
        pltpu.make_async_copy(dn.at[r, a], dr.at[r, a], dsem.at[0, r, 0]).start()
        return c

    def dn_wait(r):
        def one(d, c):
            t = lax.rem(a + d, PEERS)
            f = lax.rem(a + PEERS - d, PEERS)
            remote(dn.at[r, t], dr.at[r, f], dsem.at[0, r, d], dsem.at[1, r, d], (lead, 4 * t + q)).wait()
            return c

        lax.fori_loop(1, PEERS, one, 0)
        pltpu.make_async_copy(dn.at[r, a], dr.at[r, a], dsem.at[0, r, 0]).wait()

    dn_send(0, 0)
    dn_send(3, 0)
    dn_send(1, 0)
    dn_send(2, 0)

    xp[:, 0:8, :] = jnp.zeros((ROWS + 2, 8, D), F32)
    xp[:, COLS + 8 : COLS + 16, :] = jnp.zeros((ROWS + 2, 8, D), F32)
    dpad[:, 0:8, :] = jnp.zeros((ROWS + 2, 8, D), F32)
    dpad[:, COLS + 8 : COLS + 16, :] = jnp.zeros((ROWS + 2, 8, D), F32)

    def widen(r, c):
        xp[r + 1, 8 : COLS + 8, :] = latent[r].astype(F32)
        return c

    lax.fori_loop(0, ROWS, widen, 0)
    xp[0, 8 : COLS + 8, :] = halo[0].astype(F32)
    xp[ROWS + 1, 8 : COLS + 8, :] = halo[1].astype(F32)
    ksum[...] = jnp.zeros((9, 8, D), F32)
    tsum[...] = jnp.zeros((2, 8, D), F32)

    def fold(t):
        total = t[0:8]
        for n in range(8, CHUNK, 8):
            total = total + t[n : n + 8]
        return total

    def norm_row(r):
        dn_wait(r)
        dnf[...] = dot(perm[...], dr[r].reshape(COLS, D), 1, 0)

        def chunk(c, carry):
            at = pl.multiple_of(c * CHUNK, CHUNK)
            here = pl.ds(at, CHUNK)
            dv = dnf[here, :]
            n = nf[r, here, :]
            iv = inv[r, here, 0:1]
            tsum[0] += fold(dv * n)
            tsum[1] += fold(dv)
            g = dv * (1.0 + mod[0:1, :])
            m1 = jnp.mean(g, axis=-1, keepdims=True)
            m2 = jnp.mean(g * n, axis=-1, keepdims=True)
            res = cot[r, here, :].astype(F32) + iv * (g - m1 - n * m2)
            dpad[r + 1, pl.ds(at + 8, CHUNK), :] = res
            return carry

        lax.fori_loop(0, COLS // CHUNK, chunk, 0)

    def kernel_row(r):
        def chunk(c, carry):
            at = pl.multiple_of(c * CHUNK, CHUNK)
            w = dpad[r + 1, pl.ds(at, CHUNK + 16), :]
            dj = [w[9 - j : 9 - j + CHUNK] for j in range(3)]
            for m in range(3):
                xw = xp[r + m, pl.ds(at + 8, CHUNK), :]
                for j in range(3):
                    ksum[3 * m + j] += fold(xw * dj[j])
            return carry

        lax.fori_loop(0, COLS // CHUNK, chunk, 0)

    def out_row(r):
        def chunk(c, carry):
            at = pl.multiple_of(c * CHUNK, CHUNK)
            w = [dpad[r + m, pl.ds(at, CHUNK + 16), :] for m in range(3)]
            k = [ck[m : m + 1, :] for m in range(9)]
            t = [k[8 - j] * w[0] + k[5 - j] * w[1] + k[2 - j] * w[2] for j in range(3)]
            res = w[1][8 : CHUNK + 8] + (
                t[0][7 : CHUNK + 7] + t[1][8 : CHUNK + 8] + t[2][9 : CHUNK + 9]
            )
            gx[r, pl.ds(at, CHUNK), :] = res.astype(BF16)
            return carry

        lax.fori_loop(0, COLS // CHUNK, chunk, 0)

    orders = ("xyz", "yzx", "zxy", "xzy")

    def stage_copies(k, part, waits):
        axis = orders[part][k]
        for d in range(1, 4):
            j = ahead(axis, d)
            if k == 0:
                src = a0.at[part, pl.ds(pl.multiple_of(j * 64, 64), 64), :]
                dst = r1.at[part, d - 1]
            elif k == 1:
                src = a1.at[part, pl.ds(pl.multiple_of(j * 16, 16), 16), :]
                dst = r2.at[part, d - 1]
            else:
                src = a2.at[part, :, pl.ds(pl.multiple_of(j * 128, 128), 128)]
                dst = r3.at[part, d - 1]
            n = 2 + (k * 4 + part) * 6 + (d - 1) * 2
            cp = remote(src, dst, rsem.at[n], rsem.at[n + 1], at_axis(axis, j))
            if waits:
                cp.wait()
            else:
                cp.start()

    def stage_sum(k, part):
        axis = orders[part][k]
        m = coord[axis]
        if k == 0:
            own = a0[part, pl.ds(pl.multiple_of(m * 64, 64), 64), :]
            got, dst = r1, a1
        elif k == 1:
            own = a1[part, pl.ds(pl.multiple_of(m * 16, 16), 16), :]
            got, dst = r2, a2
        else:
            own = a2[part, :, pl.ds(pl.multiple_of(m * 128, 128), 128)]
            got, dst = r3, a3
        t = own.astype(F32)
        for d in range(3):
            t = t + got[part, d].astype(F32)
        dst[part] = t.astype(BF16)

    def stage_start(k):
        for part in range(4):
            stage_copies(k, part, False)

    def stage_end(k):
        for part in range(4):
            stage_copies(k, part, True)
            stage_sum(k, part)

    def block(part, k, values):
        rows = 0
        if k == 0:
            return total.at[core, part, pl.ds(pl.multiple_of(values[0] * 64, 64), 64), :]
        rows = pl.multiple_of(values[0] * 64 + values[1] * 16, 16)
        if k == 1:
            return total.at[core, part, pl.ds(rows, 16), :]
        return total.at[
            core, part, pl.ds(rows, 16), pl.ds(pl.multiple_of(values[2] * 128, 128), 128)
        ]

    def gather_copies(k, part, waits):
        axis = orders[part][k]
        mine = [coord[ax] for ax in orders[part]]
        for d in range(1, 4):
            src = block(part, k, mine)
            n = (k * 4 + part) * 6 + (d - 1) * 2
            if waits:
                theirs = list(mine)
                theirs[k] = behind(axis, d)
                dst = block(part, k, theirs)
            else:
                dst = src
            cp = remote(src, dst, gsem.at[n], gsem.at[n + 1], at_axis(axis, ahead(axis, d)))
            if waits:
                cp.wait()
            else:
                cp.start()

    def gather_start(k):
        for part in range(4):
            if k == 2:
                mine = [coord[ax] for ax in orders[part]]
                rows = pl.multiple_of(mine[0] * 64 + mine[1] * 16, 16)
                cols = pl.multiple_of(mine[2] * 128, 128)
                total[core, part, pl.ds(rows, 16), pl.ds(cols, 128)] = a3[part]
            gather_copies(k, part, False)

    def gather_end(k):
        for part in range(4):
            gather_copies(k, part, True)

    def twin_gather(dst):
        return remote(total.at[core], total.at[dst], rsem.at[74], rsem.at[75], twin)

    def small_copies(slots, axis, k, waits):
        m = coord[axis]
        for d in range(1, 4):
            n = (k * 3 + d - 1) * 2
            dst = slots.at[behind(axis, d)] if waits else slots.at[m]
            cp = remote(slots.at[m], dst, ssem.at[n], ssem.at[n + 1], at_axis(axis, ahead(axis, d)))
            if waits:
                cp.wait()
            else:
                cp.start()

    swap().wait()
    for part in range(4):
        def add_half(c, carry, part=part):
            rows = pl.ds(pl.multiple_of(c * 64, 64), 64)
            a0[part, rows, :] = (grads[core, part, rows, :].astype(F32) + r0[part, rows, :].astype(F32)).astype(BF16)
            return carry
        lax.fori_loop(0, 4, add_half, 0)
        stage_copies(0, part, False)

    norm_row(0)

    def halo_up():
        return remote(hsend.at[0], hrecv.at[1], hsem.at[0], hsem.at[2], (lead, space - 1))

    def halo_down():
        return remote(hsend.at[1], hrecv.at[0], hsem.at[1], hsem.at[3], (lead, space + 1))

    hsend[0] = dpad[1, 8 : COLS + 8, :].astype(BF16)

    @pl.when(space > 0)
    def _():
        halo_up().start()

    norm_row(3)
    hsend[1] = dpad[4, 8 : COLS + 8, :].astype(BF16)

    @pl.when(space < 31)
    def _():
        halo_down().start()

    stage_end(0)
    stage_start(1)
    norm_row(1)
    norm_row(2)
    stage_end(1)
    stage_start(2)

    def kernel_rows(r, c):
        kernel_row(r)
        return c

    lax.fori_loop(0, ROWS, kernel_rows, 0)
    stage_end(2)
    gather_start(2)
    for n in range(9):
        sm[n : n + 1, :] = jnp.sum(ksum[n], axis=0, keepdims=True)
    for n in range(2):
        sm[9 + n : 10 + n, :] = jnp.sum(tsum[n], axis=0, keepdims=True)
    sm[11:12, :] = leadrow[0:1, :]
    sm[12:16, :] = jnp.zeros((4, D), F32)
    s1[z] = sm[...]
    small_copies(s1, "z", 0, False)
    out_row(1)
    gather_end(2)
    gather_start(1)
    small_copies(s1, "z", 0, True)
    s2[y] = s1[0] + s1[1] + s1[2] + s1[3]
    small_copies(s2, "y", 1, False)
    out_row(2)
    gather_end(1)
    gather_start(0)
    small_copies(s2, "y", 1, True)
    s3[x] = s2[0] + s2[1] + s2[2] + s2[3]
    small_copies(s3, "x", 2, False)

    @pl.when(space > 0)
    def _():
        halo_up().wait_send()
        remote(hsend.at[1], hrecv.at[0], hsem.at[1], hsem.at[3], (lead, space - 1)).wait_recv()

    @pl.when(space < 31)
    def _():
        halo_down().wait_send()
        remote(hsend.at[0], hrecv.at[1], hsem.at[0], hsem.at[2], (lead, space + 1)).wait_recv()

    dpad[0, 8 : COLS + 8, :] = hrecv[0].astype(F32)
    dpad[ROWS + 1, 8 : COLS + 8, :] = hrecv[1].astype(F32)
    out_row(0)
    out_row(3)
    small_copies(s3, "x", 2, True)
    s4[core, 0] = s3[0] + s3[2]
    s4[core, 1] = s3[1] + s3[3]

    def small_twin(dst):
        return remote(s4.at[core], s4.at[dst], ssem.at[18], ssem.at[19], twin)

    small_twin(core).start()
    gather_end(0)
    twin_gather(core).start()
    small_twin(1 - core).wait()
    small[...] = s4[...]
    twin_gather(1 - core).wait()


def vmem(count):
    return [pl.BlockSpec(memory_space=pltpu.VMEM)] * count


def per_device(latent, lead_index, conv_kernel, cond_table, w_qkv, w_out, cotangent):
    leads = cond_table.shape[0]
    norm_scale = 1.0 / math.sqrt(4 * 128 * 256)
    field = latent[0]
    cot = cotangent[0]
    ck = conv_kernel.reshape(9, D)
    mod = lax.dynamic_index_in_dim(cond_table, lead_index[0], 0, keepdims=False)
    shape = jax.ShapeDtypeStruct
    any_spec = pl.BlockSpec(memory_space=pl.ANY)
    params = functools.partial(
        pltpu.CompilerParams, has_side_effects=True, vmem_limit_bytes=VMEM_LIMIT
    )
    dma = pltpu.SemaphoreType.DMA

    xg, cg, nf, inv, halo = pl.pallas_call(
        forward_kernel,
        out_shape=[
            shape((ROWS, PEERS, CHUNK, D), BF16),
            shape((ROWS, PEERS, CHUNK, D), BF16),
            shape((ROWS, COLS, D), F32),
            shape((ROWS, COLS, 128), F32),
            shape((2, COLS, D), BF16),
        ],
        in_specs=vmem(4),
        out_specs=[any_spec, any_spec] + vmem(3),
        scratch_shapes=[
            pltpu.VMEM((ROWS + 2, COLS + 16, D), F32),
            pltpu.VMEM((ROWS, PEERS, CHUNK, D), BF16),
            pltpu.VMEM((ROWS, PEERS, CHUNK, D), BF16),
            pltpu.VMEM((COLS, D), BF16),
            pltpu.VMEM((COLS, COLS), BF16),
            dma((4,)),
            dma((2, ROWS, PEERS)),
            dma((2, ROWS, PEERS)),
            dma((2,)),
        ],
        compiler_params=params(collective_id=1),
        name="forward",
    )(field, cot, ck, mod)

    dn, grads = pl.pallas_call(
        attention_kernel,
        out_shape=[shape((ROWS, PEERS, CHUNK, D), BF16), shape((2, 4, 256, D), BF16)],
        in_specs=vmem(4),
        out_specs=vmem(2),
        scratch_shapes=[
            pltpu.VMEM((ROWS * COLS, D), BF16),
            pltpu.VMEM((ROWS * COLS, D), BF16),
            pltpu.VMEM((COLS, 3 * D), BF16),
            pltpu.VMEM((COLS, D), BF16),
            pltpu.VMEM((ROWS * COLS, D), BF16),
            pltpu.VMEM((ROWS * COLS, 3 * D), BF16),
            pltpu.VMEM((COLS, COLS), BF16),
        ],
        compiler_params=pltpu.CompilerParams(vmem_limit_bytes=VMEM_LIMIT),
        name="attention",
    )(xg, cg, w_qkv, w_out)

    leadrow = jnp.broadcast_to(lead_index[0].astype(F32) * (1.0 / 32.0), (8, D))
    grad_x, total, small = pl.pallas_call(
        backward_kernel,
        out_shape=[
            shape((ROWS, COLS, D), BF16),
            shape((2, 4, 256, D), BF16),
            shape((2, 2, 16, D), F32),
        ],
        in_specs=vmem(10),
        out_specs=vmem(3),
        scratch_shapes=[
            pltpu.VMEM((ROWS, PEERS, CHUNK, D), BF16),
            pltpu.VMEM((COLS, D), F32),
            pltpu.VMEM((ROWS + 2, COLS + 16, D), F32),
            pltpu.VMEM((ROWS + 2, COLS + 16, D), F32),
            pltpu.VMEM((2, COLS, D), BF16),
            pltpu.VMEM((2, COLS, D), BF16),
            pltpu.VMEM((COLS, COLS), BF16),
            pltpu.VMEM((4, 256, D), BF16),
            pltpu.VMEM((4, 3, 64, D), BF16),
            pltpu.VMEM((4, 3, 16, D), BF16),
            pltpu.VMEM((4, 3, 16, 128), BF16),
            pltpu.VMEM((4, 256, D), BF16),
            pltpu.VMEM((4, 64, D), BF16),
            pltpu.VMEM((4, 16, D), BF16),
            pltpu.VMEM((4, 16, 128), BF16),
            pltpu.VMEM((9, 8, D), F32),
            pltpu.VMEM((2, 8, D), F32),
            pltpu.VMEM((16, D), F32),
            pltpu.VMEM((4, 16, D), F32),
            pltpu.VMEM((4, 16, D), F32),
            pltpu.VMEM((4, 16, D), F32),
            pltpu.VMEM((2, 2, 16, D), F32),
            dma((2, ROWS, PEERS)),
            dma((4,)),
            dma((76,)),
            dma((72,)),
            dma((20,)),
        ],
        compiler_params=params(collective_id=2),
        name="backward",
    )(dn, grads, nf, inv, mod, cot, field, halo, ck, leadrow)

    whole = total.astype(F32) * norm_scale
    grad_qkv = whole[:, :3].transpose(0, 2, 1, 3).reshape(D, 3 * D)
    grad_out = whole[:, 3].reshape(D, D)
    rows = small.reshape(4, 16, D)
    grad_kernel = (jnp.sum(rows[:, :9], axis=0) * norm_scale).reshape(3, 3, D)
    index = jnp.round(rows[:, 11, 0]).astype(jnp.int32)
    hot = jnp.arange(leads, dtype=jnp.int32)[:, None, None]
    grad_table = jnp.zeros((leads, 2, D), F32)
    for n in range(4):
        grad_table = grad_table + jnp.where(hot == index[n], rows[n, 9:11][None], 0.0)
    return (grad_x[None], grad_qkv, grad_out, grad_kernel, grad_table * norm_scale)


def solution(mesh):
    in_specs = (
        P("lead", "space", None, None),
        P("lead"),
        P(),
        P(),
        P(),
        P(),
        P("lead", "space", None, None),
    )
    out_specs = (P("lead", "space", None, None), P(), P(), P(), P())
    return jax.shard_map(
        per_device, mesh=mesh, in_specs=in_specs, out_specs=out_specs, check_vma=False
    )
```

```python
import functools
import math

import jax
import jax.numpy as jnp
from jax import lax
from jax.experimental import pallas as pl
from jax.experimental.pallas import tpu as pltpu
from jax.sharding import PartitionSpec as P

HDIM = 32
GRID = 8
EPSILON = 1e-05
ROWS = 4
COLS = 256
D = 512
PEERS = 8
CHUNK = 32
MESH = pl.DeviceIdType.MESH
F32 = jnp.float32
BF16 = jnp.bfloat16
VMEM_LIMIT = 52 * 1024 * 1024


def remote(src, dst, send, recv, device):
    return pltpu.make_async_remote_copy(
        src_ref=src, dst_ref=dst, send_sem=send, recv_sem=recv, device_id=device, device_id_type=MESH
    )


def dot(a, b, ca, cb):
    return lax.dot_general(a, b, (((ca,), (cb,)), ((), ())), preferred_element_type=F32)


def send_order():
    p = lax.broadcasted_iota(jnp.int32, (COLS, COLS), 0)
    col = lax.broadcasted_iota(jnp.int32, (COLS, COLS), 1)
    return jnp.where((p & 7) * 32 + (p >> 5) * 4 + ((p >> 3) & 3) == col, 1.0, 0.0).astype(BF16)


def field_order():
    p = lax.broadcasted_iota(jnp.int32, (COLS, COLS), 1)
    col = lax.broadcasted_iota(jnp.int32, (COLS, COLS), 0)
    return jnp.where((p & 7) * 32 + (p >> 5) * 4 + ((p >> 3) & 3) == col, 1.0, 0.0).astype(BF16)


def group_order():
    g = lax.broadcasted_iota(jnp.int32, (COLS, COLS), 0)
    p = lax.broadcasted_iota(jnp.int32, (COLS, COLS), 1)
    return jnp.where(((g >> 3) & 7) * 32 + (g >> 6) * 8 + (g & 7) == p, 1.0, 0.0).astype(BF16)


def attention_row(x, c, wqkv, wout, xg, cg, qkv, da, att, dp, perm, i):
    scale = 1.0 / math.sqrt(HDIM)
    c2 = scale * math.log2(math.e)
    base = pl.multiple_of(i * COLS, COLS)
    here = pl.ds(base, COLS)
    gx = dot(perm[...], x, 1, 0).astype(BF16)
    gc = dot(perm[...], c, 1, 0).astype(BF16)
    xg[here, :] = gx
    cg[here, :] = gc
    for n in range(3):
        qkv[:, n * D : (n + 1) * D] = dot(gx, wqkv[:, n * D : (n + 1) * D], 1, 0).astype(BF16)
    da[...] = dot(gc, wout[...], 1, 1).astype(BF16)
    lane = lax.broadcasted_iota(jnp.int32, (1, 128), 1) // HDIM
    masks16 = [jnp.where(lane == h, 1.0, 0.0).astype(BF16) for h in range(4)]
    lanes = lax.broadcasted_iota(jnp.int32, (64, 128), 1) // HDIM
    picks = [lanes == h for h in range(3)]

    def spread(t):
        return jnp.concatenate([t * m for m in masks16], axis=0)

    def gather(t):
        total = jnp.where(picks[2], t[128:192], t[192:256])
        total = jnp.where(picks[1], t[64:128], total)
        return jnp.where(picks[0], t[0:64], total)

    def group(g, carry):
        rows = pl.ds(pl.multiple_of(g * 64, 64), 64)
        out = pl.ds(pl.multiple_of(base + g * 64, 64), 64)
        at = [(t * 128, t * 128 + 128) for t in range(4)]
        qs = [spread(qkv[rows, lo:hi]) for lo, hi in at]
        k = [qkv[rows, D + lo : D + hi] for lo, hi in at]
        v = [qkv[rows, 2 * D + lo : 2 * D + hi] for lo, hi in at]
        ds_ = [spread(da[rows, lo:hi]) for lo, hi in at]
        s = [dot(a, b, 1, 1) for a, b in zip(k, qs)]
        dpr = [dot(a, b, 1, 1) for a, b in zip(v, ds_)]
        m = [jnp.max(a, axis=0, keepdims=True) * c2 for a in s]
        e = [jnp.exp2(a * c2 - b) for a, b in zip(s, m)]
        p = [a * (1.0 / jnp.sum(a, axis=0, keepdims=True)) for a in e]
        p16 = [a.astype(BF16) for a in p]
        inner = [jnp.sum(a * b, axis=0, keepdims=True) for a, b in zip(p, dpr)]
        dsc = [(a * (b - c)).astype(BF16) for a, b, c in zip(p, dpr, inner)]
        o1 = [dot(a, b, 0, 0) for a, b in zip(p16, v)]
        o2 = [dot(a, b, 1, 0) for a, b in zip(p16, ds_)]
        o3 = [dot(a, b, 0, 0) for a, b in zip(dsc, k)]
        o4 = [dot(a, b, 1, 0) for a, b in zip(dsc, qs)]
        for n, (lo, hi) in enumerate(at):
            att[out, lo:hi] = gather(o1[n]).astype(BF16)
            dp[out, 2 * D + lo : 2 * D + hi] = o2[n].astype(BF16)
            dp[out, lo:hi] = (gather(o3[n]) * scale).astype(BF16)
            dp[out, D + lo : D + hi] = (o4[n] * scale).astype(BF16)
        return carry

    lax.fori_loop(0, 4, group, 0)


def normed_back(dp, wqkv, i):
    here = pl.ds(pl.multiple_of(i * COLS, COLS), COLS)
    dnf = dot(dp[here, :], wqkv[...], 1, 1)
    blocks = [dnf[g * 64 + m * 8 : g * 64 + m * 8 + 8] for m in range(8) for g in range(4)]
    return jnp.concatenate(blocks, axis=0).astype(BF16).reshape(PEERS, CHUNK, D)


def weight_grads(xg, cg, att, dp, grads, h):
    half = pl.ds(pl.multiple_of(h * 256, 256), 256)
    for n in range(3):
        grads[h, :, n * D : (n + 1) * D] = dot(xg[:, half], dp[:, n * D : (n + 1) * D], 0, 0).astype(BF16)
    grads[h, :, 3 * D :] = dot(att[:, half], cg[...], 0, 0).astype(BF16)


PARTS = ((0, 640, "xyz"), (640, 640, "yzx"), (1280, 768, "zxy"))


def section_kernel(
    latent_any, cot_any, ck, mod, wqkv_any, wout_any, leadrow,
    gx, total, small,
    latent, cot, wqkv, wout, halo, xp, dpad, nf, inv, nrm, fperm, gperm, bperm,
    xs, cs, xr, cr, xg, cg, qkv, da, att, dp, dn, dr, dnf, hsend, hrecv,
    grads, r0, a0, r1, a1, r2, ex, ksum, tsum, sm, s1, s2, s3, s4,
    lsem, hsem, xsem, csem, dsem, bsem, wsem, rsem, gsem, ssem,
):
    lead = lax.axis_index("lead")
    space = lax.axis_index("space")
    a, q = space // 4, lax.rem(space, 4)
    core, x_lo = lax.rem(lead, 2), lead // 2
    z, y, x_hi = space // 8, lax.rem(space // 2, 4), lax.rem(space, 2)
    x = x_hi * 2 + x_lo
    coord = {"x": x, "y": y, "z": z}

    def at_axis(axis, j):
        if axis == "x":
            return ((lax.rem(j, 2) * 2 + core), space - x_hi + j // 2)
        if axis == "y":
            return (lead, space + (j - y) * 2)
        return (lead, space + (j - z) * 8)

    def ahead(axis, d):
        return lax.rem(coord[axis] + d, 4)

    def behind(axis, d):
        return lax.rem(coord[axis] + 4 - d, 4)

    twin = (lead + 1 - 2 * core, space)
    has_low, has_high = space > 0, space < 31

    loads = [
        pltpu.make_async_copy(src, dst, lsem.at[n])
        for n, (src, dst) in enumerate(
            ((latent_any, latent), (cot_any, cot), (wqkv_any, wqkv), (wout_any, wout))
        )
    ]
    for load in loads:
        load.start()

    @pl.when(space == 0)
    def _():
        halo[0] = jnp.zeros((COLS, D), BF16)
        hrecv[0] = jnp.zeros((COLS, D), BF16)

    @pl.when(space == 31)
    def _():
        halo[1] = jnp.zeros((COLS, D), BF16)
        hrecv[1] = jnp.zeros((COLS, D), BF16)

    barrier = pltpu.get_barrier_semaphore()

    def greet(device):
        pl.semaphore_signal(barrier, inc=1, device_id=device, device_id_type=MESH)

    def greet_peer(d, c):
        greet((lead, 4 * lax.rem(a + d, PEERS) + q))
        return c

    lax.fori_loop(1, PEERS, greet_peer, 0)
    for axis in "xyz":
        for d in range(1, 4):
            greet(at_axis(axis, ahead(axis, d)))
    greet(twin)

    @pl.when(has_low)
    def _():
        greet((lead, space - 1))

    @pl.when(has_high)
    def _():
        greet((lead, space + 1))

    fperm[...] = send_order()
    gperm[...] = group_order()
    bperm[...] = field_order()
    xp[:, 0:8, :] = jnp.zeros((ROWS + 2, 8, D), F32)
    xp[:, COLS + 8 : COLS + 16, :] = jnp.zeros((ROWS + 2, 8, D), F32)
    dpad[:, 0:8, :] = jnp.zeros((ROWS + 2, 8, D), F32)
    dpad[:, COLS + 8 : COLS + 16, :] = jnp.zeros((ROWS + 2, 8, D), F32)
    ksum[...] = jnp.zeros((9, 8, D), F32)
    tsum[...] = jnp.zeros((2, 8, D), F32)
    loads[0].wait()
    loads[1].wait()
    pl.semaphore_wait(barrier, 17 + jnp.where(has_low, 1, 0) + jnp.where(has_high, 1, 0))

    def edge_start(low, high, sem):
        @pl.when(has_low)
        def _():
            if low is not None:
                remote(low[0], low[1].at[1], sem.at[0], sem.at[2], (lead, space - 1)).start()

        @pl.when(has_high)
        def _():
            if high is not None:
                remote(high[0], high[1].at[0], sem.at[1], sem.at[3], (lead, space + 1)).start()

    def edge_wait(first, last, dst, sem):
        @pl.when(has_low)
        def _():
            remote(first, dst.at[1], sem.at[0], sem.at[2], (lead, space - 1)).wait_send()
            remote(last, dst.at[0], sem.at[1], sem.at[3], (lead, space - 1)).wait_recv()

        @pl.when(has_high)
        def _():
            remote(last, dst.at[0], sem.at[1], sem.at[3], (lead, space + 1)).wait_send()
            remote(first, dst.at[1], sem.at[0], sem.at[2], (lead, space + 1)).wait_recv()

    edge_start((latent.at[0], halo), (latent.at[3], halo), hsem)

    def send(bufs, out, sem, r):
        def one(d, c):
            t = lax.rem(a + d, PEERS)
            remote(bufs.at[r, t], out.at[r, a], sem.at[0, r, d], sem.at[1, r, d], (lead, 4 * t + q)).start()
            return c

        lax.fori_loop(1, PEERS, one, 0)
        pltpu.make_async_copy(bufs.at[r, a], out.at[r, a], sem.at[0, r, 0]).start()

    def finish(bufs, out, sem, r):
        def one(d, c):
            t = lax.rem(a + d, PEERS)
            f = lax.rem(a + PEERS - d, PEERS)
            remote(bufs.at[r, t], out.at[r, f], sem.at[0, r, d], sem.at[1, r, d], (lead, 4 * t + q)).wait()
            return c

        lax.fori_loop(1, PEERS, one, 0)
        pltpu.make_async_copy(bufs.at[r, a], out.at[r, a], sem.at[0, r, 0]).wait()

    def cot_row(r):
        cs[r] = dot(fperm[...], cot[r], 1, 0).astype(BF16).reshape(PEERS, CHUNK, D)
        send(cs, cr, csem, r)

    def norm_row(r):
        def chunk(c, carry):
            at = pl.multiple_of(c * CHUNK, CHUNK)
            w = [xp[r + m, pl.ds(at, CHUNK + 16), :] for m in range(3)]
            k = [ck[m : m + 1, :] for m in range(9)]
            t = [k[j] * w[0] + k[3 + j] * w[1] + k[6 + j] * w[2] for j in range(3)]
            res = w[1][8 : CHUNK + 8] + (
                t[0][7 : CHUNK + 7] + t[1][8 : CHUNK + 8] + t[2][9 : CHUNK + 9]
            )
            cen = res - jnp.mean(res, axis=-1, keepdims=True)
            iv = lax.rsqrt(jnp.mean(cen * cen, axis=-1, keepdims=True) + EPSILON)
            n = cen * iv
            nf[r, pl.ds(at, CHUNK), :] = n
            inv[r, pl.ds(at, CHUNK), :] = jnp.broadcast_to(iv, (CHUNK, 128))
            nrm[pl.ds(at, CHUNK), :] = (n * (1.0 + mod[0:1, :]) + mod[1:2, :]).astype(BF16)
            return carry

        lax.fori_loop(0, COLS // CHUNK, chunk, 0)
        xs[r] = dot(fperm[...], nrm[...], 1, 0).astype(BF16).reshape(PEERS, CHUNK, D)
        send(xs, xr, xsem, r)

    def fold(t):
        total = t[0:8]
        for n in range(8, CHUNK, 8):
            total = total + t[n : n + 8]
        return total

    def back_row(r):
        finish(dn, dr, dsem, r)
        dnf[...] = dot(bperm[...], dr[r].reshape(COLS, D), 1, 0)

        def chunk(c, carry):
            at = pl.multiple_of(c * CHUNK, CHUNK)
            here = pl.ds(at, CHUNK)
            dv = dnf[here, :]
            n = nf[r, here, :]
            iv = inv[r, here, 0:1]
            tsum[0] += fold(dv * n)
            tsum[1] += fold(dv)
            g = dv * (1.0 + mod[0:1, :])
            m1 = jnp.mean(g, axis=-1, keepdims=True)
            m2 = jnp.mean(g * n, axis=-1, keepdims=True)
            res = cot[r, here, :].astype(F32) + iv * (g - m1 - n * m2)
            dpad[r + 1, pl.ds(at + 8, CHUNK), :] = res
            return carry

        lax.fori_loop(0, COLS // CHUNK, chunk, 0)

    def kernel_rows(first, last):
        def chunk(i, carry):
            r = i // (COLS // CHUNK)
            at = pl.multiple_of(lax.rem(i, COLS // CHUNK) * CHUNK, CHUNK)
            w = dpad[r + 1, pl.ds(at, CHUNK + 16), :]
            dj = [w[9 - j : 9 - j + CHUNK] for j in range(3)]
            for m in range(3):
                xw = xp[r + m, pl.ds(at + 8, CHUNK), :]
                for j in range(3):
                    ksum[3 * m + j] += fold(xw * dj[j])
            return carry

        lax.fori_loop(first * (COLS // CHUNK), last * (COLS // CHUNK), chunk, 0)

    def out_row(r):
        def chunk(c, carry):
            at = pl.multiple_of(c * CHUNK, CHUNK)
            w = [dpad[r + m, pl.ds(at, CHUNK + 16), :] for m in range(3)]
            k = [ck[m : m + 1, :] for m in range(9)]
            t = [k[8 - j] * w[0] + k[5 - j] * w[1] + k[2 - j] * w[2] for j in range(3)]
            res = w[1][8 : CHUNK + 8] + (
                t[0][7 : CHUNK + 7] + t[1][8 : CHUNK + 8] + t[2][9 : CHUNK + 9]
            )
            gx[r, pl.ds(at, CHUNK), :] = res.astype(BF16)
            return carry

        lax.fori_loop(0, COLS // CHUNK, chunk, 0)

    def span(part):
        first, width, _ = PARTS[part]
        return slice(first, first + width)

    def swap(part):
        cols = span(part)
        return remote(
            grads.at[1 - core, :, cols], r0.at[:, cols], bsem.at[0, part], bsem.at[1, part], twin
        )

    def swap_end(part):
        cols = span(part)
        swap(part).wait()

        def add(c, carry):
            rows = pl.ds(pl.multiple_of(c * 32, 32), 32)
            a0[rows, cols] = (grads[core, rows, cols].astype(F32) + r0[rows, cols].astype(F32)).astype(BF16)
            return carry

        lax.fori_loop(0, 8, add, 0)

    def stage(k, part, waits):
        first, width, axes = PARTS[part]
        axis = axes[k]
        for d in range(1, 4):
            j = ahead(axis, d)
            if k == 0:
                src = a0.at[pl.ds(pl.multiple_of(j * 64, 64), 64), span(part)]
                dst = r1.at[part, d - 1, :, 0:width]
            elif k == 1:
                src = a1.at[part, pl.ds(pl.multiple_of(j * 16, 16), 16), 0:width]
                dst = r2.at[part, d - 1, :, 0:width]
            else:
                src = ex.at[part, coord[axis], :, 0:width]
                dst = ex.at[part, behind(axis, d) if waits else coord[axis], :, 0:width]
            cp = remote(src, dst, rsem.at[0, k, part, d], rsem.at[1, k, part, d], at_axis(axis, j))
            if waits:
                cp.wait()
            else:
                cp.start()

    def stage_start(k):
        for part in range(3):
            stage(k, part, False)

    def stage_end(k, part):
        first, width, axes = PARTS[part]
        stage(k, part, True)
        m = coord[axes[k]]
        if k == 0:
            t = a0[pl.ds(pl.multiple_of(m * 64, 64), 64), span(part)].astype(F32)
            for d in range(3):
                t = t + r1[part, d, :, 0:width].astype(F32)
            a1[part, :, 0:width] = t.astype(BF16)
        elif k == 1:
            t = a1[part, pl.ds(pl.multiple_of(m * 16, 16), 16), 0:width].astype(F32)
            for d in range(3):
                t = t + r2[part, d, :, 0:width].astype(F32)
            ex[part, coord[axes[2]], :, 0:width] = t.astype(BF16)
        else:
            t = ex[part, 0, :, 0:width].astype(F32)
            for d in range(1, 4):
                t = t + ex[part, d, :, 0:width].astype(F32)
            rows = pl.multiple_of(coord[axes[0]] * 64 + coord[axes[1]] * 16, 16)
            total[core, pl.ds(rows, 16), span(part)] = t.astype(BF16)

    def block(k, part, values):
        if k == 0:
            return total.at[core, pl.ds(pl.multiple_of(values[0] * 64, 64), 64), span(part)]
        return total.at[core, pl.ds(pl.multiple_of(values[0] * 64 + values[1] * 16, 16), 16), span(part)]

    def gather(k, part, waits):
        axes = PARTS[part][2]
        mine = [coord[ax] for ax in axes]
        for d in range(1, 4):
            theirs = list(mine)
            theirs[k] = behind(axes[k], d)
            src = block(k, part, mine)
            dst = block(k, part, theirs) if waits else src
            cp = remote(src, dst, gsem.at[0, k, part, d], gsem.at[1, k, part, d], at_axis(axes[k], ahead(axes[k], d)))
            if waits:
                cp.wait()
            else:
                cp.start()

    def twin_gather(part, waits):
        dst = total.at[(1 - core) if waits else core, :, span(part)]
        cp = remote(total.at[core, :, span(part)], dst, bsem.at[0, 3 + part], bsem.at[1, 3 + part], twin)
        if waits:
            cp.wait()
        else:
            cp.start()

    def small_stage(slots, axis, k, waits):
        m = coord[axis]
        for d in range(1, 4):
            dst = slots.at[behind(axis, d)] if waits else slots.at[m]
            cp = remote(slots.at[m], dst, ssem.at[0, k, d], ssem.at[1, k, d], at_axis(axis, ahead(axis, d)))
            if waits:
                cp.wait()
            else:
                cp.start()

    def small_twin(dst):
        return remote(s4.at[core], s4.at[dst], ssem.at[0, 3, 0], ssem.at[1, 3, 0], twin)

    def widen(r, c):
        xp[r + 1, 8 : COLS + 8, :] = latent[r].astype(F32)
        return c

    cot_row(1)
    lax.fori_loop(0, ROWS, widen, 0)

    def inner_row(i, c):
        norm_row(1 + i)

        @pl.when(i == 0)
        def _():
            cot_row(2)

        return c

    lax.fori_loop(0, 2, inner_row, 0)
    cot_row(0)
    loads[2].wait()
    loads[3].wait()

    def edge_row(i, c):
        norm_row(3 * i)

        @pl.when(i == 0)
        def _():
            cot_row(3)

        return c

    def step(i, c):
        r = jnp.where(i < 2, i + 1, (i - 2) * 3)
        finish(cs, cr, csem, r)
        finish(xs, xr, xsem, r)
        attention_row(
            xr[r].reshape(COLS, D), cr[r].reshape(COLS, D), wqkv, wout, xg, cg, qkv, da, att, dp, gperm, r
        )
        dn[r] = normed_back(dp, wqkv, r)
        send(dn, dr, dsem, r)

        @pl.when(i == 0)
        def _():
            edge_wait(latent.at[0], latent.at[3], halo, hsem)
            xp[0, 8 : COLS + 8, :] = halo[0].astype(F32)
            xp[ROWS + 1, 8 : COLS + 8, :] = halo[1].astype(F32)
            lax.fori_loop(0, 2, edge_row, 0)

        return c

    lax.fori_loop(0, ROWS, step, 0)
    weight_grads(xg, cg, att, dp, grads, 1 - core)
    for part in range(3):
        swap(part).start()
    weight_grads(xg, cg, att, dp, grads, core)
    for part in range(3):
        swap_end(part)
        stage(0, part, False)
    back_row(0)
    hsend[0] = dpad[1, 8 : COLS + 8, :].astype(BF16)
    edge_start((hsend.at[0], hrecv), None, wsem)
    back_row(3)
    hsend[1] = dpad[4, 8 : COLS + 8, :].astype(BF16)
    edge_start(None, (hsend.at[1], hrecv), wsem)
    for part in range(3):
        stage_end(0, part)
        stage(1, part, False)
    back_row(1)
    back_row(2)
    for part in range(3):
        stage_end(1, part)
        stage(2, part, False)
    kernel_rows(0, 4)
    for n in range(9):
        sm[n : n + 1, :] = jnp.sum(ksum[n], axis=0, keepdims=True)
    for n in range(2):
        sm[9 + n : 10 + n, :] = jnp.sum(tsum[n], axis=0, keepdims=True)
    sm[11:12, :] = leadrow[0:1, :]
    sm[12:16, :] = jnp.zeros((4, D), F32)
    s1[z] = sm[...]
    small_stage(s1, "z", 0, False)
    for part in range(3):
        stage_end(2, part)
        gather(1, part, False)
    out_row(1)
    out_row(2)
    small_stage(s1, "z", 0, True)
    s2[y] = s1[0] + s1[1] + s1[2] + s1[3]
    small_stage(s2, "y", 1, False)
    for part in range(3):
        gather(1, part, True)
        gather(0, part, False)
    edge_wait(hsend.at[0], hsend.at[1], hrecv, wsem)
    dpad[0, 8 : COLS + 8, :] = hrecv[0].astype(F32)
    dpad[ROWS + 1, 8 : COLS + 8, :] = hrecv[1].astype(F32)
    out_row(0)
    small_stage(s2, "y", 1, True)
    s3[x] = s2[0] + s2[1] + s2[2] + s2[3]
    small_stage(s3, "x", 2, False)
    out_row(3)
    for part in range(3):
        gather(0, part, True)
        twin_gather(part, False)
    small_stage(s3, "x", 2, True)
    s4[core, 0] = s3[0] + s3[2]
    s4[core, 1] = s3[1] + s3[3]
    small_twin(core).start()
    small_twin(1 - core).wait()
    small[...] = s4[...]
    for part in range(3):
        twin_gather(part, True)


STEPS = 4


def finish_kernel(norm_scale, table_rows, total, small, grad_qkv, grad_out, grad_kernel, grad_table):
    step = pl.program_id(0)
    whole = total[0].astype(F32) * norm_scale
    grad_qkv[...] = whole[:, : 3 * D]
    grad_out[...] = whole[:, 3 * D :]
    for n in range(9):
        row = small[0, n : n + 1, :]
        for m in range(1, 4):
            row = row + small[m, n : n + 1, :]
        grad_kernel[n // 3, n % 3 : n % 3 + 1, :] = row * norm_scale
    grad_table[...] = jnp.zeros(grad_table.shape, F32)
    for m in range(4):
        index = (jnp.max(small[m, 11:12, 0:128]) + 0.5).astype(jnp.int32) - step * table_rows

        @pl.when((index >= 0) & (index < table_rows))
        def _():
            grad_table[index] = grad_table[index] + small[m, 9:11, :] * norm_scale


def vmem(count):
    return [pl.BlockSpec(memory_space=pltpu.VMEM)] * count


def per_device(latent, lead_index, conv_kernel, cond_table, w_qkv, w_out, cotangent):
    leads = cond_table.shape[0]
    norm_scale = 1.0 / math.sqrt(4 * 128 * 256)
    ck = conv_kernel.reshape(9, D)
    mod = lax.dynamic_index_in_dim(cond_table, lead_index[0], 0, keepdims=False)
    leadrow = jnp.broadcast_to(lead_index[0].astype(F32) * (1.0 / 32.0), (8, D))
    shape = jax.ShapeDtypeStruct
    far = pl.BlockSpec(memory_space=pl.ANY)
    near = pl.BlockSpec(memory_space=pltpu.VMEM)
    dma = pltpu.SemaphoreType.DMA
    f32 = lambda *dims: pltpu.VMEM(dims, F32)
    bf16 = lambda *dims: pltpu.VMEM(dims, BF16)
    blocks = (ROWS, PEERS, CHUNK, D)

    grad_x, total, small = pl.pallas_call(
        section_kernel,
        out_shape=[
            shape((ROWS, COLS, D), BF16),
            shape((2, 256, 4 * D), BF16),
            shape((2, 2, 16, D), F32),
        ],
        in_specs=[far, far, near, near, far, far, near],
        out_specs=[near, near, near],
        scratch_shapes=[
            bf16(ROWS, COLS, D),
            bf16(ROWS, COLS, D),
            bf16(D, 3 * D),
            bf16(D, D),
            bf16(2, COLS, D),
            f32(ROWS + 2, COLS + 16, D),
            f32(ROWS + 2, COLS + 16, D),
            f32(ROWS, COLS, D),
            f32(ROWS, COLS, 128),
            bf16(COLS, D),
            bf16(COLS, COLS),
            bf16(COLS, COLS),
            bf16(COLS, COLS),
            bf16(*blocks),
            bf16(*blocks),
            bf16(*blocks),
            bf16(*blocks),
            bf16(ROWS * COLS, D),
            bf16(ROWS * COLS, D),
            bf16(COLS, 3 * D),
            bf16(COLS, D),
            bf16(ROWS * COLS, D),
            bf16(ROWS * COLS, 3 * D),
            bf16(*blocks),
            bf16(*blocks),
            f32(COLS, D),
            bf16(2, COLS, D),
            bf16(2, COLS, D),
            bf16(2, 256, 4 * D),
            bf16(256, 4 * D),
            bf16(256, 4 * D),
            bf16(3, 3, 64, 768),
            bf16(3, 64, 768),
            bf16(3, 3, 16, 768),
            bf16(3, 4, 16, 768),
            f32(9, 8, D),
            f32(2, 8, D),
            f32(16, D),
            f32(4, 16, D),
            f32(4, 16, D),
            f32(4, 16, D),
            f32(2, 2, 16, D),
            dma((4,)),
            dma((4,)),
            dma((2, ROWS, PEERS)),
            dma((2, ROWS, PEERS)),
            dma((2, ROWS, PEERS)),
            dma((2, 6)),
            dma((4,)),
            dma((2, 3, 3, 4)),
            dma((2, 2, 3, 4)),
            dma((2, 4, 4)),
        ],
        compiler_params=pltpu.CompilerParams(
            collective_id=1, has_side_effects=True, vmem_limit_bytes=VMEM_LIMIT
        ),
        name="section",
    )(latent[0], cotangent[0], ck, mod, w_qkv, w_out, leadrow)

    table_rows = -(-leads // STEPS)
    grad_qkv, grad_out, grad_kernel, grad_table = pl.pallas_call(
        functools.partial(finish_kernel, norm_scale, table_rows),
        grid=(STEPS,),
        out_shape=[
            shape((D, 3 * D), F32),
            shape((D, D), F32),
            shape((3, 3, D), F32),
            shape((leads, 2, D), F32),
        ],
        in_specs=[
            pl.BlockSpec((1, 512 // STEPS, 4 * D), lambda i: (i // 2, i % 2, 0)),
            pl.BlockSpec((4, 16, D), lambda i: (0, 0, 0)),
        ],
        out_specs=[
            pl.BlockSpec((512 // STEPS, 3 * D), lambda i: (i, 0)),
            pl.BlockSpec((512 // STEPS, D), lambda i: (i, 0)),
            pl.BlockSpec((3, 3, D), lambda i: (0, 0, 0)),
            pl.BlockSpec((table_rows, 2, D), lambda i: (i, 0, 0)),
        ],
        compiler_params=pltpu.CompilerParams(vmem_limit_bytes=VMEM_LIMIT),
        name="finish",
    )(total, small.reshape(4, 16, D))
    return (grad_x[None], grad_qkv, grad_out, grad_kernel, grad_table)


def solution(mesh):
    in_specs = (
        P("lead", "space", None, None),
        P("lead"),
        P(),
        P(),
        P(),
        P(),
        P("lead", "space", None, None),
    )
    out_specs = (P("lead", "space", None, None), P(), P(), P(), P())
    return jax.shard_map(
        per_device, mesh=mesh, in_specs=in_specs, out_specs=out_specs, check_vma=False
    )
```

```python
import functools
import math

import jax
import jax.numpy as jnp
from jax import lax
from jax.experimental import pallas as pl
from jax.experimental.pallas import tpu as pltpu
from jax.sharding import PartitionSpec as P

HDIM = 32
GRID = 8
EPSILON = 1e-05
ROWS = 4
COLS = 256
D = 512
PEERS = 8
CHUNK = 32
MESH = pl.DeviceIdType.MESH
F32 = jnp.float32
BF16 = jnp.bfloat16
VMEM_LIMIT = 61 * 1024 * 1024


def remote(src, dst, send, recv, device):
    return pltpu.make_async_remote_copy(
        src_ref=src, dst_ref=dst, send_sem=send, recv_sem=recv, device_id=device, device_id_type=MESH
    )


def dot(a, b, ca, cb):
    return lax.dot_general(a, b, (((ca,), (cb,)), ((), ())), preferred_element_type=F32)


def send_order():
    p = lax.broadcasted_iota(jnp.int32, (COLS, COLS), 0)
    col = lax.broadcasted_iota(jnp.int32, (COLS, COLS), 1)
    return jnp.where((p & 7) * 32 + (p >> 5) * 4 + ((p >> 3) & 3) == col, 1.0, 0.0).astype(BF16)


def field_order():
    p = lax.broadcasted_iota(jnp.int32, (COLS, COLS), 1)
    col = lax.broadcasted_iota(jnp.int32, (COLS, COLS), 0)
    return jnp.where((p & 7) * 32 + (p >> 5) * 4 + ((p >> 3) & 3) == col, 1.0, 0.0).astype(BF16)


def group_order():
    g = lax.broadcasted_iota(jnp.int32, (COLS, COLS), 0)
    p = lax.broadcasted_iota(jnp.int32, (COLS, COLS), 1)
    return jnp.where(((g >> 3) & 7) * 32 + (g >> 6) * 8 + (g & 7) == p, 1.0, 0.0).astype(BF16)


def attention_row(x, c, wqkv, wout, xg, cg, qkv, da, att, dp, perm, i):
    scale = 1.0 / math.sqrt(HDIM)
    c2 = scale * math.log2(math.e)
    base = pl.multiple_of(i * COLS, COLS)
    here = pl.ds(base, COLS)
    gx = dot(perm[...], x, 1, 0).astype(BF16)
    gc = dot(perm[...], c, 1, 0).astype(BF16)
    xg[here, :] = gx
    cg[here, :] = gc
    for n in range(3):
        qkv[:, n * D : (n + 1) * D] = dot(gx, wqkv[:, n * D : (n + 1) * D], 1, 0).astype(BF16)
    da[...] = dot(gc, wout[...], 1, 1).astype(BF16)
    lane = lax.broadcasted_iota(jnp.int32, (1, 128), 1) // HDIM
    masks16 = [jnp.where(lane == h, 1.0, 0.0).astype(BF16) for h in range(4)]
    lanes = lax.broadcasted_iota(jnp.int32, (64, 128), 1) // HDIM
    picks = [lanes == h for h in range(3)]

    def spread(t):
        return jnp.concatenate([t * m for m in masks16], axis=0)

    def gather(t):
        total = jnp.where(picks[2], t[128:192], t[192:256])
        total = jnp.where(picks[1], t[64:128], total)
        return jnp.where(picks[0], t[0:64], total)

    def group(g, carry):
        rows = pl.ds(pl.multiple_of(g * 64, 64), 64)
        out = pl.ds(pl.multiple_of(base + g * 64, 64), 64)
        at = [(t * 128, t * 128 + 128) for t in range(4)]
        qs = [spread(qkv[rows, lo:hi]) for lo, hi in at]
        k = [qkv[rows, D + lo : D + hi] for lo, hi in at]
        v = [qkv[rows, 2 * D + lo : 2 * D + hi] for lo, hi in at]
        ds_ = [spread(da[rows, lo:hi]) for lo, hi in at]
        s = [dot(a, b, 1, 1) for a, b in zip(k, qs)]
        dpr = [dot(a, b, 1, 1) for a, b in zip(v, ds_)]
        m = [jnp.max(a, axis=0, keepdims=True) * c2 for a in s]
        e = [jnp.exp2(a * c2 - b) for a, b in zip(s, m)]
        p = [a * (1.0 / jnp.sum(a, axis=0, keepdims=True)) for a in e]
        p16 = [a.astype(BF16) for a in p]
        inner = [jnp.sum(a * b, axis=0, keepdims=True) for a, b in zip(p, dpr)]
        dsc = [(a * (b - c)).astype(BF16) for a, b, c in zip(p, dpr, inner)]
        o1 = [dot(a, b, 0, 0) for a, b in zip(p16, v)]
        o2 = [dot(a, b, 1, 0) for a, b in zip(p16, ds_)]
        o3 = [dot(a, b, 0, 0) for a, b in zip(dsc, k)]
        o4 = [dot(a, b, 1, 0) for a, b in zip(dsc, qs)]
        for n, (lo, hi) in enumerate(at):
            att[out, lo:hi] = gather(o1[n]).astype(BF16)
            dp[out, 2 * D + lo : 2 * D + hi] = o2[n].astype(BF16)
            dp[out, lo:hi] = (gather(o3[n]) * scale).astype(BF16)
            dp[out, D + lo : D + hi] = (o4[n] * scale).astype(BF16)
        return carry

    lax.fori_loop(0, 4, group, 0)


def normed_back(dp, wqkv, i):
    here = pl.ds(pl.multiple_of(i * COLS, COLS), COLS)
    dnf = dot(dp[here, :], wqkv[...], 1, 1)
    blocks = [dnf[g * 64 + m * 8 : g * 64 + m * 8 + 8] for m in range(8) for g in range(4)]
    return jnp.concatenate(blocks, axis=0).astype(BF16).reshape(PEERS, CHUNK, D)


def grads_of(xg, cg, att, dp, here, half, n):
    if n < 3:
        return dot(xg[here, half], dp[here, n * D : (n + 1) * D], 0, 0)
    return dot(att[here, half], cg[here, :], 0, 0)


def add_grads(xg, cg, att, dp, acc, i):
    here = pl.ds(pl.multiple_of(i * COLS, COLS), COLS)
    for h in range(2):
        for n in range(4):
            half = slice(h * 256, h * 256 + 256)
            acc[h, :, n * D : (n + 1) * D] += grads_of(xg, cg, att, dp, here, half, n)


PARTS = ((0, 640, "xyz"), (640, 640, "yzx"), (1280, 768, "zxy"))
NP = len(PARTS)
WIDE = 768


def section_kernel(
    latent_any, cot_any, ck, lead_index, cond_any, wqkv_any, wout_any,
    gx_any, total_any, small,
    gx, total, latent, cot, wqkv, wout, cond, mod, halo, xp, dpad, nf, inv, nrm, fperm, gperm, bperm,
    xs, cs, xr, cr, xg, cg, qkv, da, att, dp, dn, dr, dnf, hsend, hrecv,
    acc, grads, r0, a0, r1, a1, r2, ex, ksum, tsum, sm, s1, s2, s3, s4,
    lsem, hsem, xsem, csem, dsem, bsem, wsem, rsem, gsem, ssem, osem,
):
    lead = lax.axis_index("lead")
    space = lax.axis_index("space")
    a, q = space // 4, lax.rem(space, 4)
    core, x_lo = lax.rem(lead, 2), lead // 2
    z, y, x_hi = space // 8, lax.rem(space // 2, 4), lax.rem(space, 2)
    x = x_hi * 2 + x_lo
    coord = {"x": x, "y": y, "z": z}

    def at_axis(axis, j):
        if axis == "x":
            return ((lax.rem(j, 2) * 2 + core), space - x_hi + j // 2)
        if axis == "y":
            return (lead, space + (j - y) * 2)
        return (lead, space + (j - z) * 8)

    def ahead(axis, d):
        return lax.rem(coord[axis] + d, 4)

    def behind(axis, d):
        return lax.rem(coord[axis] + 4 - d, 4)

    twin = (lead + 1 - 2 * core, space)
    has_low, has_high = space > 0, space < 31

    loads = [
        pltpu.make_async_copy(src, dst, lsem.at[n])
        for n, (src, dst) in enumerate(
            (
                (cot_any.at[1], cot.at[1]),
                (latent_any.at[0:2], latent.at[0:2]),
                (latent_any.at[2:4], latent.at[2:4]),
                (cond_any, cond),
                (cot_any.at[2:4], cot.at[2:4]),
                (cot_any.at[0], cot.at[0]),
                (wqkv_any, wqkv),
                (wout_any, wout),
            )
        )
    ]
    for load in loads:
        load.start()

    @pl.when(space == 0)
    def _():
        halo[0] = jnp.zeros((COLS, D), BF16)
        hrecv[0] = jnp.zeros((COLS, D), BF16)

    @pl.when(space == 31)
    def _():
        halo[1] = jnp.zeros((COLS, D), BF16)
        hrecv[1] = jnp.zeros((COLS, D), BF16)

    barrier = pltpu.get_barrier_semaphore()

    def greet(device):
        pl.semaphore_signal(barrier, inc=1, device_id=device, device_id_type=MESH)

    def greet_peer(d, c):
        greet((lead, 4 * lax.rem(a + d, PEERS) + q))
        return c

    lax.fori_loop(1, PEERS, greet_peer, 0)
    for axis in "xyz":
        for d in range(1, 4):
            greet(at_axis(axis, ahead(axis, d)))
    greet(twin)

    @pl.when(has_low)
    def _():
        greet((lead, space - 1))

    @pl.when(has_high)
    def _():
        greet((lead, space + 1))

    fperm[...] = send_order()
    pl.semaphore_wait(barrier, 17 + jnp.where(has_low, 1, 0) + jnp.where(has_high, 1, 0))

    def edge(src, dst, piece, sem, up):
        cells = slice(piece * 128, piece * 128 + 128)
        n = 2 * piece + (0 if up else 4)
        device = (lead, space - 1) if up else (lead, space + 1)
        return remote(src.at[cells], dst.at[1 if up else 0, cells], sem.at[n], sem.at[n + 1], device)

    def edge_start(src, dst, piece, sem, up):
        @pl.when(has_low if up else has_high)
        def _():
            edge(src, dst, piece, sem, up).start()

    def edge_wait(first, last, dst, sem):
        for piece in range(2):

            @pl.when(has_low)
            def _():
                edge(first, dst, piece, sem, True).wait_send()
                edge(last, dst, piece, sem, False).wait_recv()

            @pl.when(has_high)
            def _():
                edge(last, dst, piece, sem, False).wait_send()
                edge(first, dst, piece, sem, True).wait_recv()

    for piece in range(2):
        edge_start(latent_any.at[0], halo, piece, hsem, True)
        edge_start(latent_any.at[3], halo, piece, hsem, False)

    def send(bufs, out, sem, r):
        def one(d, c):
            t = lax.rem(a + d, PEERS)
            remote(bufs.at[r, t], out.at[r, a], sem.at[0, r, d], sem.at[1, r, d], (lead, 4 * t + q)).start()
            return c

        lax.fori_loop(1, PEERS, one, 0)
        pltpu.make_async_copy(bufs.at[r, a], out.at[r, a], sem.at[0, r, 0]).start()

    def finish(bufs, out, sem, r):
        def one(d, c):
            t = lax.rem(a + d, PEERS)
            f = lax.rem(a + PEERS - d, PEERS)
            remote(bufs.at[r, t], out.at[r, f], sem.at[0, r, d], sem.at[1, r, d], (lead, 4 * t + q)).wait()
            return c

        lax.fori_loop(1, PEERS, one, 0)
        pltpu.make_async_copy(bufs.at[r, a], out.at[r, a], sem.at[0, r, 0]).wait()

    def cot_row(r):
        cs[r] = dot(fperm[...], cot[r], 1, 0).astype(BF16).reshape(PEERS, CHUNK, D)
        send(cs, cr, csem, r)

    def norm_row(r):
        def chunk(c, carry):
            at = pl.multiple_of(c * CHUNK, CHUNK)
            w = [xp[r + m, pl.ds(at, CHUNK + 16), :] for m in range(3)]
            k = [ck[m // 3, m % 3 : m % 3 + 1, :] for m in range(9)]
            t = [k[j] * w[0] + k[3 + j] * w[1] + k[6 + j] * w[2] for j in range(3)]
            res = w[1][8 : CHUNK + 8] + (
                t[0][7 : CHUNK + 7] + t[1][8 : CHUNK + 8] + t[2][9 : CHUNK + 9]
            )
            cen = res - jnp.mean(res, axis=-1, keepdims=True)
            iv = lax.rsqrt(jnp.mean(cen * cen, axis=-1, keepdims=True) + EPSILON)
            n = cen * iv
            nf[r, pl.ds(at, CHUNK), :] = n
            inv[r, pl.ds(at, CHUNK), :] = jnp.broadcast_to(iv, (CHUNK, 128))
            nrm[pl.ds(at, CHUNK), :] = (n * (1.0 + mod[0:1, :]) + mod[1:2, :]).astype(BF16)
            return carry

        lax.fori_loop(0, COLS // CHUNK, chunk, 0)
        xs[r] = dot(fperm[...], nrm[...], 1, 0).astype(BF16).reshape(PEERS, CHUNK, D)

    def fold(t):
        total = t[0:8]
        for n in range(8, CHUNK, 8):
            total = total + t[n : n + 8]
        return total

    def back_row(r):
        finish(dn, dr, dsem, r)
        dnf[...] = dot(bperm[...], dr[r].reshape(COLS, D), 1, 0)

        def chunk(c, carry):
            at = pl.multiple_of(c * CHUNK, CHUNK)
            here = pl.ds(at, CHUNK)
            dv = dnf[here, :]
            n = nf[r, here, :]
            iv = inv[r, here, 0:1]
            tsum[0] += fold(dv * n)
            tsum[1] += fold(dv)
            g = dv * (1.0 + mod[0:1, :])
            m1 = jnp.mean(g, axis=-1, keepdims=True)
            m2 = jnp.mean(g * n, axis=-1, keepdims=True)
            res = cot[r, here, :].astype(F32) + iv * (g - m1 - n * m2)
            dpad[r + 1, pl.ds(at + 8, CHUNK), :] = res
            return carry

        lax.fori_loop(0, COLS // CHUNK, chunk, 0)

    def kernel_rows(first, last):
        def chunk(i, carry):
            r = i // (COLS // CHUNK)
            at = pl.multiple_of(lax.rem(i, COLS // CHUNK) * CHUNK, CHUNK)
            w = dpad[r + 1, pl.ds(at, CHUNK + 16), :]
            dj = [w[9 - j : 9 - j + CHUNK] for j in range(3)]
            for m in range(3):
                xw = xp[r + m, pl.ds(at + 8, CHUNK), :]
                for j in range(3):
                    ksum[3 * m + j] += fold(xw * dj[j])
            return carry

        lax.fori_loop(first * (COLS // CHUNK), last * (COLS // CHUNK), chunk, 0)

    def out_row(r):
        def chunk(c, carry):
            at = pl.multiple_of(c * CHUNK, CHUNK)
            w = [dpad[r + m, pl.ds(at, CHUNK + 16), :] for m in range(3)]
            k = [ck[m // 3, m % 3 : m % 3 + 1, :] for m in range(9)]
            t = [k[8 - j] * w[0] + k[5 - j] * w[1] + k[2 - j] * w[2] for j in range(3)]
            res = w[1][8 : CHUNK + 8] + (
                t[0][7 : CHUNK + 7] + t[1][8 : CHUNK + 8] + t[2][9 : CHUNK + 9]
            )
            gx[r, pl.ds(at, CHUNK), :] = res.astype(BF16)
            return carry

        lax.fori_loop(0, COLS // CHUNK, chunk, 0)
        keep_row(r).start()

    def span(part):
        first, width, _ = PARTS[part]
        return slice(first, first + width)

    def swap(part):
        cols = span(part)
        return remote(
            grads.at[:, cols], r0.at[:, cols], bsem.at[0, part], bsem.at[1, part], twin
        )

    def swap_end(part):
        cols = span(part)
        swap(part).wait()

        def add(c, carry):
            rows = pl.ds(pl.multiple_of(c * 32, 32), 32)
            a0[rows, cols] = (acc[core, rows, cols] + r0[rows, cols].astype(F32)).astype(BF16)
            return carry

        lax.fori_loop(0, 8, add, 0)

    def stage(k, part, waits):
        first, width, axes = PARTS[part]
        axis = axes[k]
        for d in range(1, 4):
            j = ahead(axis, d)
            if k == 0:
                src = a0.at[pl.ds(pl.multiple_of(j * 64, 64), 64), span(part)]
                dst = r1.at[part, d - 1, :, 0:width]
            elif k == 1:
                src = a1.at[part, pl.ds(pl.multiple_of(j * 16, 16), 16), 0:width]
                dst = r2.at[part, d - 1, :, 0:width]
            else:
                src = ex.at[part, coord[axis], :, 0:width]
                dst = ex.at[part, behind(axis, d) if waits else coord[axis], :, 0:width]
            cp = remote(src, dst, rsem.at[0, k, part, d], rsem.at[1, k, part, d], at_axis(axis, j))
            if waits:
                cp.wait()
            else:
                cp.start()

    def stage_start(k):
        for part in range(NP):
            stage(k, part, False)

    def stage_end(k, part):
        first, width, axes = PARTS[part]
        stage(k, part, True)
        m = coord[axes[k]]
        if k == 0:
            t = a0[pl.ds(pl.multiple_of(m * 64, 64), 64), span(part)].astype(F32)
            for d in range(3):
                t = t + r1[part, d, :, 0:width].astype(F32)
            a1[part, :, 0:width] = t.astype(BF16)
        elif k == 1:
            t = a1[part, pl.ds(pl.multiple_of(m * 16, 16), 16), 0:width].astype(F32)
            for d in range(3):
                t = t + r2[part, d, :, 0:width].astype(F32)
            ex[part, coord[axes[2]], :, 0:width] = t.astype(BF16)
        else:
            t = ex[part, 0, :, 0:width].astype(F32)
            for d in range(1, 4):
                t = t + ex[part, d, :, 0:width].astype(F32)
            rows = pl.multiple_of(coord[axes[0]] * 64 + coord[axes[1]] * 16, 16)
            total[pl.ds(rows, 16), span(part)] = t.astype(BF16)

    def block(k, part, values):
        if k == 0:
            return total.at[pl.ds(pl.multiple_of(values[0] * 64, 64), 64), span(part)]
        return total.at[pl.ds(pl.multiple_of(values[0] * 64 + values[1] * 16, 16), 16), span(part)]

    def gather(k, part, waits):
        axes = PARTS[part][2]
        mine = [coord[ax] for ax in axes]
        for d in range(1, 4):
            theirs = list(mine)
            theirs[k] = behind(axes[k], d)
            src = block(k, part, mine)
            dst = block(k, part, theirs) if waits else src
            cp = remote(src, dst, gsem.at[0, k, part, d], gsem.at[1, k, part, d], at_axis(axes[k], ahead(axes[k], d)))
            if waits:
                cp.wait()
            else:
                cp.start()

    def keep(part):
        return pltpu.make_async_copy(
            total.at[:, span(part)], total_any.at[core, :, span(part)], osem.at[part]
        )

    def twin_gather(part, waits):
        keep(part).wait() if waits else keep(part).start()
        dst = total_any.at[(1 - core) if waits else core, :, span(part)]
        cp = remote(total.at[:, span(part)], dst, bsem.at[0, NP + part], bsem.at[1, NP + part], twin)
        if waits:
            cp.wait()
        else:
            cp.start()

    def keep_row(r):
        return pltpu.make_async_copy(gx.at[r], gx_any.at[r], osem.at[NP + r])

    def small_stage(slots, axis, k, waits):
        m = coord[axis]
        for d in range(1, 4):
            dst = slots.at[behind(axis, d)] if waits else slots.at[m]
            cp = remote(slots.at[m], dst, ssem.at[0, k, d], ssem.at[1, k, d], at_axis(axis, ahead(axis, d)))
            if waits:
                cp.wait()
            else:
                cp.start()

    def small_twin(dst):
        return remote(s4.at[core], s4.at[dst], ssem.at[0, 3, 0], ssem.at[1, 3, 0], twin)

    def widen(r, c):
        xp[r + 1, 8 : COLS + 8, :] = latent[r].astype(F32)
        return c

    loads[0].wait()
    cot_row(1)
    xp[:, 0:8, :] = jnp.zeros((ROWS + 2, 8, D), F32)
    xp[:, COLS + 8 : COLS + 16, :] = jnp.zeros((ROWS + 2, 8, D), F32)
    loads[1].wait()
    loads[2].wait()
    lax.fori_loop(0, ROWS, widen, 0)
    loads[3].wait()
    mod[...] = cond[lead_index[0]]
    loads[4].wait()

    def inner_row(i, c):
        norm_row(1 + i)
        send(xs, xr, xsem, 1 + i)

        @pl.when(i == 0)
        def _():
            cot_row(2)

        return c

    lax.fori_loop(0, 2, inner_row, 0)
    loads[5].wait()
    cot_row(0)
    cot_row(3)
    gperm[...] = group_order()
    bperm[...] = field_order()
    dpad[:, 0:8, :] = jnp.zeros((ROWS + 2, 8, D), F32)
    dpad[:, COLS + 8 : COLS + 16, :] = jnp.zeros((ROWS + 2, 8, D), F32)
    ksum[...] = jnp.zeros((9, 8, D), F32)
    tsum[...] = jnp.zeros((2, 8, D), F32)
    acc[...] = jnp.zeros(acc.shape, F32)
    loads[6].wait()
    loads[7].wait()

    def edge_row(i, c):
        norm_row(3 * i)
        send(xs, xr, xsem, 3 * i)
        return c

    def step(i, c):
        r = jnp.where(i < 2, i + 1, (i - 2) * 3)
        finish(cs, cr, csem, r)
        finish(xs, xr, xsem, r)
        attention_row(
            xr[r].reshape(COLS, D), cr[r].reshape(COLS, D), wqkv, wout, xg, cg, qkv, da, att, dp, gperm, i
        )

        @pl.when(i == 0)
        def _():
            edge_wait(latent_any.at[0], latent_any.at[3], halo, hsem)
            xp[0, 8 : COLS + 8, :] = halo[0].astype(F32)
            xp[ROWS + 1, 8 : COLS + 8, :] = halo[1].astype(F32)
            lax.fori_loop(0, 2, edge_row, 0)

        dn[r] = normed_back(dp, wqkv, i)
        send(dn, dr, dsem, r)

        @pl.when(i < 2)
        def _():
            add_grads(xg, cg, att, dp, acc, i)

        return c

    lax.fori_loop(0, ROWS, step, 0)
    late = slice(2 * COLS, 4 * COLS)
    theirs = pl.ds(pl.multiple_of((1 - core) * 256, 256), 256)
    ours = pl.ds(pl.multiple_of(core * 256, 256), 256)
    for n in range(4):
        cols = slice(n * D, (n + 1) * D)
        grads[:, cols] = (acc[1 - core, :, cols] + grads_of(xg, cg, att, dp, late, theirs, n)).astype(BF16)
    for part in range(NP):
        swap(part).start()
    for n in range(4):
        acc[core, :, n * D : (n + 1) * D] += grads_of(xg, cg, att, dp, late, ours, n)
    back_row(0)
    hsend[0] = dpad[1, 8 : COLS + 8, :].astype(BF16)
    for piece in range(2):
        edge_start(hsend.at[0], hrecv, piece, wsem, True)
    for part in range(NP):
        swap_end(part)
        stage(0, part, False)
    back_row(1)
    back_row(2)
    back_row(3)
    hsend[1] = dpad[4, 8 : COLS + 8, :].astype(BF16)
    for piece in range(2):
        edge_start(hsend.at[1], hrecv, piece, wsem, False)
    for part in range(NP):
        stage_end(0, part)
        stage(1, part, False)
    kernel_rows(0, 4)
    for n in range(9):
        sm[n : n + 1, :] = jnp.sum(ksum[n], axis=0, keepdims=True)
    for n in range(2):
        sm[9 + n : 10 + n, :] = jnp.sum(tsum[n], axis=0, keepdims=True)
    sm[11:12, :] = jnp.full((1, D), lead_index[0].astype(F32) * (1.0 / 32.0))
    sm[12:16, :] = jnp.zeros((4, D), F32)
    s1[z] = sm[...]
    small_stage(s1, "z", 0, False)
    for part in range(NP):
        stage_end(1, part)
        stage(2, part, False)
    out_row(1)
    out_row(2)
    small_stage(s1, "z", 0, True)
    s2[y] = s1[0] + s1[1] + s1[2] + s1[3]
    small_stage(s2, "y", 1, False)
    for part in range(NP):
        stage_end(2, part)
        gather(1, part, False)
    small_stage(s2, "y", 1, True)
    s3[x] = s2[0] + s2[1] + s2[2] + s2[3]
    small_stage(s3, "x", 2, False)
    for part in range(NP):
        gather(1, part, True)
        gather(0, part, False)
    edge_wait(hsend.at[0], hsend.at[1], hrecv, wsem)
    dpad[0, 8 : COLS + 8, :] = hrecv[0].astype(F32)
    dpad[ROWS + 1, 8 : COLS + 8, :] = hrecv[1].astype(F32)
    out_row(0)
    out_row(3)
    small_stage(s3, "x", 2, True)
    s4[core, 0] = s3[0] + s3[2]
    s4[core, 1] = s3[1] + s3[3]
    small_twin(core).start()
    for part in range(NP):
        gather(0, part, True)
        twin_gather(part, False)
    small_twin(1 - core).wait()
    small[...] = s4[...]
    for r in range(ROWS):
        keep_row(r).wait()
    for part in range(NP):
        twin_gather(part, True)


STEPS = 2


def finish_kernel(norm_scale, table_rows, total, small, grad_qkv, grad_out, grad_kernel, grad_table):
    step = pl.program_id(0)
    whole = total[0].astype(F32) * norm_scale
    grad_qkv[...] = whole[:, : 3 * D]
    grad_out[...] = whole[:, 3 * D :]
    for n in range(9):
        row = small[0, n : n + 1, :]
        for m in range(1, 4):
            row = row + small[m, n : n + 1, :]
        grad_kernel[n // 3, n % 3 : n % 3 + 1, :] = row * norm_scale
    grad_table[...] = jnp.zeros(grad_table.shape, F32)
    for m in range(4):
        index = (jnp.max(small[m, 11:12, 0:128]) + 0.5).astype(jnp.int32) - step * table_rows

        @pl.when((index >= 0) & (index < table_rows))
        def _():
            grad_table[index] = grad_table[index] + small[m, 9:11, :] * norm_scale


def vmem(count):
    return [pl.BlockSpec(memory_space=pltpu.VMEM)] * count


def per_device(latent, lead_index, conv_kernel, cond_table, w_qkv, w_out, cotangent):
    leads = cond_table.shape[0]
    norm_scale = 1.0 / math.sqrt(4 * 128 * 256)
    shape = jax.ShapeDtypeStruct
    far = pl.BlockSpec(memory_space=pl.ANY)
    near = pl.BlockSpec(memory_space=pltpu.VMEM)
    dma = pltpu.SemaphoreType.DMA
    f32 = lambda *dims: pltpu.VMEM(dims, F32)
    bf16 = lambda *dims: pltpu.VMEM(dims, BF16)
    blocks = (ROWS, PEERS, CHUNK, D)

    grad_x, total, small = pl.pallas_call(
        section_kernel,
        out_shape=[
            shape((ROWS, COLS, D), BF16),
            shape((2, 256, 4 * D), BF16),
            shape((2, 2, 16, D), F32),
        ],
        in_specs=[far, far, near, pl.BlockSpec(memory_space=pltpu.SMEM), far, far, far],
        out_specs=[far, far, near],
        scratch_shapes=[
            bf16(ROWS, COLS, D),
            bf16(256, 4 * D),
            bf16(ROWS, COLS, D),
            bf16(ROWS, COLS, D),
            bf16(D, 3 * D),
            bf16(D, D),
            f32(leads, 2, D),
            f32(2, D),
            bf16(2, COLS, D),
            f32(ROWS + 2, COLS + 16, D),
            f32(ROWS + 2, COLS + 16, D),
            f32(ROWS, COLS, D),
            f32(ROWS, COLS, 128),
            bf16(COLS, D),
            bf16(COLS, COLS),
            bf16(COLS, COLS),
            bf16(COLS, COLS),
            bf16(*blocks),
            bf16(*blocks),
            bf16(*blocks),
            bf16(*blocks),
            bf16(ROWS * COLS, D),
            bf16(ROWS * COLS, D),
            bf16(COLS, 3 * D),
            bf16(COLS, D),
            bf16(ROWS * COLS, D),
            bf16(ROWS * COLS, 3 * D),
            bf16(*blocks),
            bf16(*blocks),
            f32(COLS, D),
            bf16(2, COLS, D),
            bf16(2, COLS, D),
            f32(2, 256, 4 * D),
            bf16(256, 4 * D),
            bf16(256, 4 * D),
            bf16(256, 4 * D),
            bf16(NP, 3, 64, WIDE),
            bf16(NP, 64, WIDE),
            bf16(NP, 3, 16, WIDE),
            bf16(NP, 4, 16, WIDE),
            f32(9, 8, D),
            f32(2, 8, D),
            f32(16, D),
            f32(4, 16, D),
            f32(4, 16, D),
            f32(4, 16, D),
            f32(2, 2, 16, D),
            dma((8,)),
            dma((8,)),
            dma((2, ROWS, PEERS)),
            dma((2, ROWS, PEERS)),
            dma((2, ROWS, PEERS)),
            dma((2, 2 * NP)),
            dma((8,)),
            dma((2, 3, NP, 4)),
            dma((2, 2, NP, 4)),
            dma((2, 4, 4)),
            dma((NP + ROWS,)),
        ],
        compiler_params=pltpu.CompilerParams(
            collective_id=1, has_side_effects=True, vmem_limit_bytes=VMEM_LIMIT
        ),
        name="section",
    )(latent[0], cotangent[0], conv_kernel, lead_index, cond_table, w_qkv, w_out)

    table_rows = -(-leads // STEPS)
    grad_qkv, grad_out, grad_kernel, grad_table = pl.pallas_call(
        functools.partial(finish_kernel, norm_scale, table_rows),
        grid=(STEPS,),
        out_shape=[
            shape((D, 3 * D), F32),
            shape((D, D), F32),
            shape((3, 3, D), F32),
            shape((leads, 2, D), F32),
        ],
        in_specs=[
            pl.BlockSpec((1, 512 // STEPS, 4 * D), lambda i: (i, 0, 0)),
            pl.BlockSpec((4, 16, D), lambda i: (0, 0, 0)),
        ],
        out_specs=[
            pl.BlockSpec((512 // STEPS, 3 * D), lambda i: (i, 0)),
            pl.BlockSpec((512 // STEPS, D), lambda i: (i, 0)),
            pl.BlockSpec((3, 3, D), lambda i: (0, 0, 0)),
            pl.BlockSpec((table_rows, 2, D), lambda i: (i, 0, 0)),
        ],
        compiler_params=pltpu.CompilerParams(vmem_limit_bytes=VMEM_LIMIT),
        name="finish",
    )(total, small.reshape(4, 16, D))
    return (grad_x[None], grad_qkv, grad_out, grad_kernel, grad_table)


def solution(mesh):
    in_specs = (
        P("lead", "space", None, None),
        P("lead"),
        P(),
        P(),
        P(),
        P(),
        P("lead", "space", None, None),
    )
    out_specs = (P("lead", "space", None, None), P(), P(), P(), P())
    return jax.shard_map(
        per_device, mesh=mesh, in_specs=in_specs, out_specs=out_specs, check_vma=False
    )
```

```python
import functools
import math

import jax
import jax.numpy as jnp
from jax import lax
from jax.experimental import pallas as pl
from jax.experimental.pallas import tpu as pltpu
from jax.sharding import PartitionSpec as P

HDIM = 32
GRID = 8
EPSILON = 1e-05
ROWS = 4
COLS = 256
D = 512
PEERS = 8
CHUNK = 32
MESH = pl.DeviceIdType.MESH
F32 = jnp.float32
BF16 = jnp.bfloat16
VMEM_LIMIT = 61 * 1024 * 1024


def remote(src, dst, send, recv, device):
    return pltpu.make_async_remote_copy(
        src_ref=src, dst_ref=dst, send_sem=send, recv_sem=recv, device_id=device, device_id_type=MESH
    )


def dot(a, b, ca, cb):
    return lax.dot_general(a, b, (((ca,), (cb,)), ((), ())), preferred_element_type=F32)


def send_order():
    p = lax.broadcasted_iota(jnp.int32, (COLS, COLS), 0)
    col = lax.broadcasted_iota(jnp.int32, (COLS, COLS), 1)
    return jnp.where((p & 7) * 32 + (p >> 5) * 4 + ((p >> 3) & 3) == col, 1.0, 0.0).astype(BF16)


def field_order():
    p = lax.broadcasted_iota(jnp.int32, (COLS, COLS), 1)
    col = lax.broadcasted_iota(jnp.int32, (COLS, COLS), 0)
    return jnp.where((p & 7) * 32 + (p >> 5) * 4 + ((p >> 3) & 3) == col, 1.0, 0.0).astype(BF16)


def group_order():
    g = lax.broadcasted_iota(jnp.int32, (COLS, COLS), 0)
    p = lax.broadcasted_iota(jnp.int32, (COLS, COLS), 1)
    return jnp.where(((g >> 3) & 7) * 32 + (g >> 6) * 8 + (g & 7) == p, 1.0, 0.0).astype(BF16)


def attention_row(x, c, wqkv, wout, xg, cg, qkv, da, att, dp, perm, i):
    scale = 1.0 / math.sqrt(HDIM)
    c2 = scale * math.log2(math.e)
    base = pl.multiple_of(i * COLS, COLS)
    here = pl.ds(base, COLS)
    gx = dot(perm[...], x, 1, 0).astype(BF16)
    gc = dot(perm[...], c, 1, 0).astype(BF16)
    xg[here, :] = gx
    cg[here, :] = gc
    for n in range(3):
        qkv[:, n * D : (n + 1) * D] = dot(gx, wqkv[:, n * D : (n + 1) * D], 1, 0).astype(BF16)
    da[...] = dot(gc, wout[...], 1, 1).astype(BF16)
    lane = lax.broadcasted_iota(jnp.int32, (1, 128), 1) // HDIM
    masks16 = [jnp.where(lane == h, 1.0, 0.0).astype(BF16) for h in range(4)]
    lanes = lax.broadcasted_iota(jnp.int32, (64, 128), 1) // HDIM
    picks = [lanes == h for h in range(3)]

    def spread(t):
        return jnp.concatenate([t * m for m in masks16], axis=0)

    def gather(t):
        total = jnp.where(picks[2], t[128:192], t[192:256])
        total = jnp.where(picks[1], t[64:128], total)
        return jnp.where(picks[0], t[0:64], total)

    def group(g, carry):
        rows = pl.ds(pl.multiple_of(g * 64, 64), 64)
        out = pl.ds(pl.multiple_of(base + g * 64, 64), 64)
        at = [(t * 128, t * 128 + 128) for t in range(4)]
        qs = [spread(qkv[rows, lo:hi]) for lo, hi in at]
        k = [qkv[rows, D + lo : D + hi] for lo, hi in at]
        v = [qkv[rows, 2 * D + lo : 2 * D + hi] for lo, hi in at]
        ds_ = [spread(da[rows, lo:hi]) for lo, hi in at]
        s = [dot(a, b, 1, 1) for a, b in zip(k, qs)]
        dpr = [dot(a, b, 1, 1) for a, b in zip(v, ds_)]
        m = [jnp.max(a, axis=0, keepdims=True) * c2 for a in s]
        e = [jnp.exp2(a * c2 - b) for a, b in zip(s, m)]
        p = [a * (1.0 / jnp.sum(a, axis=0, keepdims=True)) for a in e]
        p16 = [a.astype(BF16) for a in p]
        inner = [jnp.sum(a * b, axis=0, keepdims=True) for a, b in zip(p, dpr)]
        dsc = [(a * (b - c)).astype(BF16) for a, b, c in zip(p, dpr, inner)]
        o1 = [dot(a, b, 0, 0) for a, b in zip(p16, v)]
        o2 = [dot(a, b, 1, 0) for a, b in zip(p16, ds_)]
        o3 = [dot(a, b, 0, 0) for a, b in zip(dsc, k)]
        o4 = [dot(a, b, 1, 0) for a, b in zip(dsc, qs)]
        for n, (lo, hi) in enumerate(at):
            att[out, lo:hi] = gather(o1[n]).astype(BF16)
            dp[out, 2 * D + lo : 2 * D + hi] = o2[n].astype(BF16)
            dp[out, lo:hi] = (gather(o3[n]) * scale).astype(BF16)
            dp[out, D + lo : D + hi] = (o4[n] * scale).astype(BF16)
        return carry

    lax.fori_loop(0, 4, group, 0)


def normed_back(dp, wqkv, i):
    here = pl.ds(pl.multiple_of(i * COLS, COLS), COLS)
    dnf = dot(dp[here, :], wqkv[...], 1, 1)
    blocks = [dnf[g * 64 + m * 8 : g * 64 + m * 8 + 8] for m in range(8) for g in range(4)]
    return jnp.concatenate(blocks, axis=0).astype(BF16).reshape(PEERS, CHUNK, D)


def grads_of(xg, cg, att, dp, here, half, n):
    if n < 3:
        return dot(xg[here, half], dp[here, n * D : (n + 1) * D], 0, 0)
    return dot(att[here, half], cg[here, :], 0, 0)


def add_grads(xg, cg, att, dp, acc, i):
    here = pl.ds(pl.multiple_of(i * COLS, COLS), COLS)
    for h in range(2):
        for n in range(4):
            half = slice(h * 256, h * 256 + 256)
            acc[h, :, n * D : (n + 1) * D] += grads_of(xg, cg, att, dp, here, half, n)


PARTS = ((0, 640, "xyz"), (640, 640, "yzx"), (1280, 768, "zxy"))
NP = len(PARTS)
WIDE = 768


def section_kernel(
    latent_any, cot_any, ck, lead_index, cond_any, wqkv_any, wout_any,
    gx_any, total_any, small,
    gx, total, latent, cot, wqkv, wout, cond, mod, halo, xp, dpad, nf, inv, nrm, fperm, gperm, bperm,
    xs, cs, xr, cr, xg, cg, qkv, da, att, dp, dn, dr, dnf, hsend, hrecv,
    acc, grads, r0, a0, r1, a1, r2, ex, ksum, tsum, sm, s1, s2, s3, s4,
    lsem, hsem, xsem, csem, dsem, bsem, wsem, rsem, gsem, ssem, osem,
):
    lead = lax.axis_index("lead")
    space = lax.axis_index("space")
    a, q = space // 4, lax.rem(space, 4)
    core, x_lo = lax.rem(lead, 2), lead // 2
    z, y, x_hi = space // 8, lax.rem(space // 2, 4), lax.rem(space, 2)
    x = x_hi * 2 + x_lo
    coord = {"x": x, "y": y, "z": z}

    def at_axis(axis, j):
        if axis == "x":
            return ((lax.rem(j, 2) * 2 + core), space - x_hi + j // 2)
        if axis == "y":
            return (lead, space + (j - y) * 2)
        return (lead, space + (j - z) * 8)

    def ahead(axis, d):
        return lax.rem(coord[axis] + d, 4)

    def behind(axis, d):
        return lax.rem(coord[axis] + 4 - d, 4)

    twin = (lead + 1 - 2 * core, space)
    has_low, has_high = space > 0, space < 31

    loads = [
        pltpu.make_async_copy(src, dst, lsem.at[n])
        for n, (src, dst) in enumerate(
            (
                (cot_any.at[1], cot.at[1]),
                (latent_any.at[0:2], latent.at[0:2]),
                (latent_any.at[2:4], latent.at[2:4]),
                (cond_any, cond),
                (cot_any.at[2:4], cot.at[2:4]),
                (cot_any.at[0], cot.at[0]),
                (wqkv_any, wqkv),
                (wout_any, wout),
            )
        )
    ]
    for load in loads:
        load.start()

    @pl.when(space == 0)
    def _():
        halo[0] = jnp.zeros((COLS, D), BF16)
        hrecv[0] = jnp.zeros((COLS, D), BF16)

    @pl.when(space == 31)
    def _():
        halo[1] = jnp.zeros((COLS, D), BF16)
        hrecv[1] = jnp.zeros((COLS, D), BF16)

    barrier = pltpu.get_barrier_semaphore()

    def greet(device):
        pl.semaphore_signal(barrier, inc=1, device_id=device, device_id_type=MESH)

    def greet_peer(d, c):
        greet((lead, 4 * lax.rem(a + d, PEERS) + q))
        return c

    lax.fori_loop(1, PEERS, greet_peer, 0)
    for axis in "xyz":
        for d in range(1, 4):
            greet(at_axis(axis, ahead(axis, d)))
    greet(twin)

    @pl.when(has_low)
    def _():
        greet((lead, space - 1))

    @pl.when(has_high)
    def _():
        greet((lead, space + 1))

    fperm[...] = send_order()
    pl.semaphore_wait(barrier, 17 + jnp.where(has_low, 1, 0) + jnp.where(has_high, 1, 0))

    def edge(src, dst, piece, sem, up):
        cells = slice(piece * 128, piece * 128 + 128)
        n = 2 * piece + (0 if up else 4)
        device = (lead, space - 1) if up else (lead, space + 1)
        return remote(src.at[cells], dst.at[1 if up else 0, cells], sem.at[n], sem.at[n + 1], device)

    def edge_start(src, dst, piece, sem, up):
        @pl.when(has_low if up else has_high)
        def _():
            edge(src, dst, piece, sem, up).start()

    def edge_wait(first, last, dst, sem):
        for piece in range(2):

            @pl.when(has_low)
            def _():
                edge(first, dst, piece, sem, True).wait_send()
                edge(last, dst, piece, sem, False).wait_recv()

            @pl.when(has_high)
            def _():
                edge(last, dst, piece, sem, False).wait_send()
                edge(first, dst, piece, sem, True).wait_recv()

    for piece in range(2):
        edge_start(latent_any.at[0], halo, piece, hsem, True)
        edge_start(latent_any.at[3], halo, piece, hsem, False)

    def send(bufs, out, sem, r):
        def one(d, c):
            t = lax.rem(a + d, PEERS)
            remote(bufs.at[r, t], out.at[r, a], sem.at[0, r, d], sem.at[1, r, d], (lead, 4 * t + q)).start()
            return c

        lax.fori_loop(1, PEERS, one, 0)
        pltpu.make_async_copy(bufs.at[r, a], out.at[r, a], sem.at[0, r, 0]).start()

    def finish(bufs, out, sem, r):
        def one(d, c):
            t = lax.rem(a + d, PEERS)
            f = lax.rem(a + PEERS - d, PEERS)
            remote(bufs.at[r, t], out.at[r, f], sem.at[0, r, d], sem.at[1, r, d], (lead, 4 * t + q)).wait()
            return c

        lax.fori_loop(1, PEERS, one, 0)
        pltpu.make_async_copy(bufs.at[r, a], out.at[r, a], sem.at[0, r, 0]).wait()

    def cot_row(r):
        cs[r] = dot(fperm[...], cot[r], 1, 0).astype(BF16).reshape(PEERS, CHUNK, D)
        send(cs, cr, csem, r)

    def norm_row(r):
        def chunk(c, carry):
            at = pl.multiple_of(c * CHUNK, CHUNK)
            w = [xp[r + m, pl.ds(at, CHUNK + 16), :] for m in range(3)]
            k = [ck[m // 3, m % 3 : m % 3 + 1, :] for m in range(9)]
            t = [k[j] * w[0] + k[3 + j] * w[1] + k[6 + j] * w[2] for j in range(3)]
            res = w[1][8 : CHUNK + 8] + (
                t[0][7 : CHUNK + 7] + t[1][8 : CHUNK + 8] + t[2][9 : CHUNK + 9]
            )
            cen = res - jnp.mean(res, axis=-1, keepdims=True)
            iv = lax.rsqrt(jnp.mean(cen * cen, axis=-1, keepdims=True) + EPSILON)
            n = cen * iv
            nf[r, pl.ds(at, CHUNK), :] = n
            inv[r, pl.ds(at, CHUNK), :] = jnp.broadcast_to(iv, (CHUNK, 128))
            nrm[pl.ds(at, CHUNK), :] = (n * (1.0 + mod[0:1, :]) + mod[1:2, :]).astype(BF16)
            return carry

        lax.fori_loop(0, COLS // CHUNK, chunk, 0)
        xs[r] = dot(fperm[...], nrm[...], 1, 0).astype(BF16).reshape(PEERS, CHUNK, D)

    def fold(t):
        total = t[0:8]
        for n in range(8, CHUNK, 8):
            total = total + t[n : n + 8]
        return total

    def back_row(r):
        finish(dn, dr, dsem, r)
        dnf[...] = dot(bperm[...], dr[r].reshape(COLS, D), 1, 0)

        def chunk(c, carry):
            at = pl.multiple_of(c * CHUNK, CHUNK)
            here = pl.ds(at, CHUNK)
            dv = dnf[here, :]
            n = nf[r, here, :]
            iv = inv[r, here, 0:1]
            tsum[0] += fold(dv * n)
            tsum[1] += fold(dv)
            g = dv * (1.0 + mod[0:1, :])
            m1 = jnp.mean(g, axis=-1, keepdims=True)
            m2 = jnp.mean(g * n, axis=-1, keepdims=True)
            res = cot[r, here, :].astype(F32) + iv * (g - m1 - n * m2)
            dpad[r + 1, pl.ds(at + 8, CHUNK), :] = res
            return carry

        lax.fori_loop(0, COLS // CHUNK, chunk, 0)

    def kernel_rows(first, last):
        def chunk(i, carry):
            r = i // (COLS // CHUNK)
            at = pl.multiple_of(lax.rem(i, COLS // CHUNK) * CHUNK, CHUNK)
            w = dpad[r + 1, pl.ds(at, CHUNK + 16), :]
            dj = [w[9 - j : 9 - j + CHUNK] for j in range(3)]
            for m in range(3):
                xw = xp[r + m, pl.ds(at + 8, CHUNK), :]
                for j in range(3):
                    ksum[3 * m + j] += fold(xw * dj[j])
            return carry

        lax.fori_loop(first * (COLS // CHUNK), last * (COLS // CHUNK), chunk, 0)

    def out_row(r):
        def chunk(c, carry):
            at = pl.multiple_of(c * CHUNK, CHUNK)
            w = [dpad[r + m, pl.ds(at, CHUNK + 16), :] for m in range(3)]
            k = [ck[m // 3, m % 3 : m % 3 + 1, :] for m in range(9)]
            t = [k[8 - j] * w[0] + k[5 - j] * w[1] + k[2 - j] * w[2] for j in range(3)]
            res = w[1][8 : CHUNK + 8] + (
                t[0][7 : CHUNK + 7] + t[1][8 : CHUNK + 8] + t[2][9 : CHUNK + 9]
            )
            gx[r, pl.ds(at, CHUNK), :] = res.astype(BF16)
            return carry

        lax.fori_loop(0, COLS // CHUNK, chunk, 0)
        keep_row(r).start()

    def span(part):
        first, width, _ = PARTS[part]
        return slice(first, first + width)

    def swap(part):
        cols = span(part)
        return remote(
            grads.at[:, cols], r0.at[:, cols], bsem.at[0, part], bsem.at[1, part], twin
        )

    def swap_end(part):
        cols = span(part)
        swap(part).wait()

        def add(c, carry):
            rows = pl.ds(pl.multiple_of(c * 32, 32), 32)
            a0[rows, cols] = (acc[core, rows, cols] + r0[rows, cols].astype(F32)).astype(BF16)
            return carry

        lax.fori_loop(0, 8, add, 0)

    def stage(k, part, waits):
        first, width, axes = PARTS[part]
        axis = axes[k]
        for d in range(1, 4):
            j = ahead(axis, d)
            if k == 0:
                src = a0.at[pl.ds(pl.multiple_of(j * 64, 64), 64), span(part)]
                dst = r1.at[part, d - 1, :, 0:width]
            elif k == 1:
                src = a1.at[part, pl.ds(pl.multiple_of(j * 16, 16), 16), 0:width]
                dst = r2.at[part, d - 1, :, 0:width]
            else:
                src = ex.at[part, coord[axis], :, 0:width]
                dst = ex.at[part, behind(axis, d) if waits else coord[axis], :, 0:width]
            cp = remote(src, dst, rsem.at[0, k, part, d], rsem.at[1, k, part, d], at_axis(axis, j))
            if waits:
                cp.wait()
            else:
                cp.start()

    def stage_start(k):
        for part in range(NP):
            stage(k, part, False)

    def stage_end(k, part):
        first, width, axes = PARTS[part]
        stage(k, part, True)
        m = coord[axes[k]]
        if k == 0:
            t = a0[pl.ds(pl.multiple_of(m * 64, 64), 64), span(part)].astype(F32)
            for d in range(3):
                t = t + r1[part, d, :, 0:width].astype(F32)
            a1[part, :, 0:width] = t.astype(BF16)
        elif k == 1:
            t = a1[part, pl.ds(pl.multiple_of(m * 16, 16), 16), 0:width].astype(F32)
            for d in range(3):
                t = t + r2[part, d, :, 0:width].astype(F32)
            ex[part, coord[axes[2]], :, 0:width] = t.astype(BF16)
        else:
            t = ex[part, 0, :, 0:width].astype(F32)
            for d in range(1, 4):
                t = t + ex[part, d, :, 0:width].astype(F32)
            rows = pl.multiple_of(coord[axes[0]] * 64 + coord[axes[1]] * 16, 16)
            total[pl.ds(rows, 16), span(part)] = t.astype(BF16)

    def block(k, part, values):
        if k == 0:
            return total.at[pl.ds(pl.multiple_of(values[0] * 64, 64), 64), span(part)]
        return total.at[pl.ds(pl.multiple_of(values[0] * 64 + values[1] * 16, 16), 16), span(part)]

    def gather(k, part, waits):
        axes = PARTS[part][2]
        mine = [coord[ax] for ax in axes]
        for d in range(1, 4):
            theirs = list(mine)
            theirs[k] = behind(axes[k], d)
            src = block(k, part, mine)
            dst = block(k, part, theirs) if waits else src
            cp = remote(src, dst, gsem.at[0, k, part, d], gsem.at[1, k, part, d], at_axis(axes[k], ahead(axes[k], d)))
            if waits:
                cp.wait()
            else:
                cp.start()

    def keep(part):
        return pltpu.make_async_copy(
            total.at[:, span(part)], total_any.at[core, :, span(part)], osem.at[part]
        )

    def twin_gather(part, waits):
        keep(part).wait() if waits else keep(part).start()
        dst = total_any.at[(1 - core) if waits else core, :, span(part)]
        cp = remote(total.at[:, span(part)], dst, bsem.at[0, NP + part], bsem.at[1, NP + part], twin)
        if waits:
            cp.wait()
        else:
            cp.start()

    def keep_row(r):
        return pltpu.make_async_copy(gx.at[r], gx_any.at[r], osem.at[NP + r])

    def small_stage(slots, axis, k, waits):
        m = coord[axis]
        for d in range(1, 4):
            dst = slots.at[behind(axis, d)] if waits else slots.at[m]
            cp = remote(slots.at[m], dst, ssem.at[0, k, d], ssem.at[1, k, d], at_axis(axis, ahead(axis, d)))
            if waits:
                cp.wait()
            else:
                cp.start()

    def small_twin(dst):
        return remote(s4.at[core], s4.at[dst], ssem.at[0, 3, 0], ssem.at[1, 3, 0], twin)

    def widen(r, c):
        xp[r + 1, 8 : COLS + 8, :] = latent[r].astype(F32)
        return c

    loads[0].wait()
    cot_row(1)
    xp[:, 0:8, :] = jnp.zeros((ROWS + 2, 8, D), F32)
    xp[:, COLS + 8 : COLS + 16, :] = jnp.zeros((ROWS + 2, 8, D), F32)
    loads[1].wait()
    loads[2].wait()
    lax.fori_loop(0, ROWS, widen, 0)
    loads[3].wait()
    mod[...] = cond[lead_index[0]]
    loads[4].wait()

    def inner_row(i, c):
        norm_row(1 + i)
        send(xs, xr, xsem, 1 + i)

        @pl.when(i == 0)
        def _():
            cot_row(2)

        return c

    lax.fori_loop(0, 2, inner_row, 0)
    loads[5].wait()
    cot_row(0)
    cot_row(3)
    gperm[...] = group_order()
    bperm[...] = field_order()
    dpad[:, 0:8, :] = jnp.zeros((ROWS + 2, 8, D), F32)
    dpad[:, COLS + 8 : COLS + 16, :] = jnp.zeros((ROWS + 2, 8, D), F32)
    ksum[...] = jnp.zeros((9, 8, D), F32)
    tsum[...] = jnp.zeros((2, 8, D), F32)
    acc[...] = jnp.zeros(acc.shape, F32)
    loads[6].wait()
    loads[7].wait()

    def edge_row(i, c):
        norm_row(3 * i)
        send(xs, xr, xsem, 3 * i)
        return c

    def step(i, c):
        r = jnp.where(i < 2, i + 1, (i - 2) * 3)

        finish(cs, cr, csem, r)
        finish(xs, xr, xsem, r)
        attention_row(
            xr[r].reshape(COLS, D), cr[r].reshape(COLS, D), wqkv, wout, xg, cg, qkv, da, att, dp, gperm, i
        )

        @pl.when(i == 0)
        def _():
            edge_wait(latent_any.at[0], latent_any.at[3], halo, hsem)
            xp[0, 8 : COLS + 8, :] = halo[0].astype(F32)
            xp[ROWS + 1, 8 : COLS + 8, :] = halo[1].astype(F32)
            lax.fori_loop(0, 2, edge_row, 0)

        dn[r] = normed_back(dp, wqkv, i)
        send(dn, dr, dsem, r)

        @pl.when(i < 2)
        def _():
            add_grads(xg, cg, att, dp, acc, i)

        return c

    lax.fori_loop(0, ROWS, step, 0)
    late = slice(2 * COLS, 4 * COLS)
    theirs = pl.ds(pl.multiple_of((1 - core) * 256, 256), 256)
    ours = pl.ds(pl.multiple_of(core * 256, 256), 256)
    for n in range(4):
        cols = slice(n * D, (n + 1) * D)
        grads[:, cols] = (acc[1 - core, :, cols] + grads_of(xg, cg, att, dp, late, theirs, n)).astype(BF16)
    for part in range(NP):
        swap(part).start()
    for n in range(4):
        acc[core, :, n * D : (n + 1) * D] += grads_of(xg, cg, att, dp, late, ours, n)
    back_row(0)
    hsend[0] = dpad[1, 8 : COLS + 8, :].astype(BF16)
    for part in range(NP):
        swap_end(part)
        stage(0, part, False)
    back_row(1)
    back_row(2)
    kernel_rows(0, 3)
    for part in range(NP):
        stage_end(0, part)
        stage(1, part, False)
    back_row(3)
    hsend[1] = dpad[4, 8 : COLS + 8, :].astype(BF16)
    kernel_rows(3, 4)
    for n in range(9):
        sm[n : n + 1, :] = jnp.sum(ksum[n], axis=0, keepdims=True)
    for n in range(2):
        sm[9 + n : 10 + n, :] = jnp.sum(tsum[n], axis=0, keepdims=True)
    sm[11:12, :] = jnp.full((1, D), lead_index[0].astype(F32) * (1.0 / 32.0))
    sm[12:16, :] = jnp.zeros((4, D), F32)
    s1[z] = sm[...]
    small_stage(s1, "z", 0, False)
    for part in range(NP):
        stage_end(1, part)
        stage(2, part, False)
    for piece in range(2):
        edge_start(hsend.at[0], hrecv, piece, wsem, True)
    out_row(1)
    out_row(2)
    small_stage(s1, "z", 0, True)
    s2[y] = s1[0] + s1[1] + s1[2] + s1[3]
    small_stage(s2, "y", 1, False)
    for part in range(NP):
        stage_end(2, part)
        gather(1, part, False)
    for piece in range(2):
        edge_start(hsend.at[1], hrecv, piece, wsem, False)
    small_stage(s2, "y", 1, True)
    s3[x] = s2[0] + s2[1] + s2[2] + s2[3]
    small_stage(s3, "x", 2, False)
    for part in range(NP):
        gather(1, part, True)
        gather(0, part, False)
    edge_wait(hsend.at[0], hsend.at[1], hrecv, wsem)
    dpad[0, 8 : COLS + 8, :] = hrecv[0].astype(F32)
    dpad[ROWS + 1, 8 : COLS + 8, :] = hrecv[1].astype(F32)
    out_row(0)
    out_row(3)
    small_stage(s3, "x", 2, True)
    s4[core, 0] = s3[0] + s3[2]
    s4[core, 1] = s3[1] + s3[3]
    small_twin(core).start()
    for part in range(NP):
        gather(0, part, True)
        twin_gather(part, False)
    small_twin(1 - core).wait()
    small[...] = s4[...]
    for r in range(ROWS):
        keep_row(r).wait()
    for part in range(NP):
        twin_gather(part, True)


STEPS = 2


def finish_kernel(
    norm_scale, table_rows, total, small, gx, grad_qkv, grad_out, grad_kernel, grad_table, grad_x
):
    step = pl.program_id(0)
    grad_x[...] = gx[...]
    whole = total[0].astype(F32) * norm_scale
    grad_qkv[...] = whole[:, : 3 * D]
    grad_out[...] = whole[:, 3 * D :]
    for n in range(9):
        row = small[0, n : n + 1, :]
        for m in range(1, 4):
            row = row + small[m, n : n + 1, :]
        grad_kernel[n // 3, n % 3 : n % 3 + 1, :] = row * norm_scale
    grad_table[...] = jnp.zeros(grad_table.shape, F32)
    for m in range(4):
        index = (jnp.max(small[m, 11:12, 0:128]) + 0.5).astype(jnp.int32) - step * table_rows

        @pl.when((index >= 0) & (index < table_rows))
        def _():
            grad_table[index] = grad_table[index] + small[m, 9:11, :] * norm_scale


def vmem(count):
    return [pl.BlockSpec(memory_space=pltpu.VMEM)] * count


def per_device(latent, lead_index, conv_kernel, cond_table, w_qkv, w_out, cotangent):
    leads = cond_table.shape[0]
    norm_scale = 1.0 / math.sqrt(4 * 128 * 256)
    shape = jax.ShapeDtypeStruct
    far = pl.BlockSpec(memory_space=pl.ANY)
    near = pl.BlockSpec(memory_space=pltpu.VMEM)
    dma = pltpu.SemaphoreType.DMA
    f32 = lambda *dims: pltpu.VMEM(dims, F32)
    bf16 = lambda *dims: pltpu.VMEM(dims, BF16)
    blocks = (ROWS, PEERS, CHUNK, D)

    grad_x, total, small = pl.pallas_call(
        section_kernel,
        out_shape=[
            shape((ROWS, COLS, D), BF16),
            shape((2, 256, 4 * D), BF16),
            shape((2, 2, 16, D), F32),
        ],
        in_specs=[far, far, near, pl.BlockSpec(memory_space=pltpu.SMEM), far, far, far],
        out_specs=[far, far, near],
        scratch_shapes=[
            bf16(ROWS, COLS, D),
            bf16(256, 4 * D),
            bf16(ROWS, COLS, D),
            bf16(ROWS, COLS, D),
            bf16(D, 3 * D),
            bf16(D, D),
            f32(leads, 2, D),
            f32(2, D),
            bf16(2, COLS, D),
            f32(ROWS + 2, COLS + 16, D),
            f32(ROWS + 2, COLS + 16, D),
            f32(ROWS, COLS, D),
            f32(ROWS, COLS, 128),
            bf16(COLS, D),
            bf16(COLS, COLS),
            bf16(COLS, COLS),
            bf16(COLS, COLS),
            bf16(*blocks),
            bf16(*blocks),
            bf16(*blocks),
            bf16(*blocks),
            bf16(ROWS * COLS, D),
            bf16(ROWS * COLS, D),
            bf16(COLS, 3 * D),
            bf16(COLS, D),
            bf16(ROWS * COLS, D),
            bf16(ROWS * COLS, 3 * D),
            bf16(*blocks),
            bf16(*blocks),
            f32(COLS, D),
            bf16(2, COLS, D),
            bf16(2, COLS, D),
            f32(2, 256, 4 * D),
            bf16(256, 4 * D),
            bf16(256, 4 * D),
            bf16(256, 4 * D),
            bf16(NP, 3, 64, WIDE),
            bf16(NP, 64, WIDE),
            bf16(NP, 3, 16, WIDE),
            bf16(NP, 4, 16, WIDE),
            f32(9, 8, D),
            f32(2, 8, D),
            f32(16, D),
            f32(4, 16, D),
            f32(4, 16, D),
            f32(4, 16, D),
            f32(2, 2, 16, D),
            dma((8,)),
            dma((8,)),
            dma((2, ROWS, PEERS)),
            dma((2, ROWS, PEERS)),
            dma((2, ROWS, PEERS)),
            dma((2, 2 * NP)),
            dma((8,)),
            dma((2, 3, NP, 4)),
            dma((2, 2, NP, 4)),
            dma((2, 4, 4)),
            dma((NP + ROWS,)),
        ],
        compiler_params=pltpu.CompilerParams(
            collective_id=1, has_side_effects=True, vmem_limit_bytes=VMEM_LIMIT
        ),
        name="section",
    )(latent[0], cotangent[0], conv_kernel, lead_index, cond_table, w_qkv, w_out)

    table_rows = -(-leads // STEPS)
    grad_qkv, grad_out, grad_kernel, grad_table, grad_x = pl.pallas_call(
        functools.partial(finish_kernel, norm_scale, table_rows),
        grid=(STEPS,),
        out_shape=[
            shape((D, 3 * D), F32),
            shape((D, D), F32),
            shape((3, 3, D), F32),
            shape((leads, 2, D), F32),
            shape((ROWS, COLS, D), BF16),
        ],
        in_specs=[
            pl.BlockSpec((1, 512 // STEPS, 4 * D), lambda i: (i, 0, 0)),
            pl.BlockSpec((4, 16, D), lambda i: (0, 0, 0)),
            pl.BlockSpec((ROWS // STEPS, COLS, D), lambda i: (i, 0, 0)),
        ],
        out_specs=[
            pl.BlockSpec((512 // STEPS, 3 * D), lambda i: (i, 0)),
            pl.BlockSpec((512 // STEPS, D), lambda i: (i, 0)),
            pl.BlockSpec((3, 3, D), lambda i: (0, 0, 0)),
            pl.BlockSpec((table_rows, 2, D), lambda i: (i, 0, 0)),
            pl.BlockSpec((ROWS // STEPS, COLS, D), lambda i: (i, 0, 0)),
        ],
        compiler_params=pltpu.CompilerParams(vmem_limit_bytes=VMEM_LIMIT),
        name="finish",
    )(total, small.reshape(4, 16, D), grad_x)
    return (grad_x[None], grad_qkv, grad_out, grad_kernel, grad_table)


def solution(mesh):
    in_specs = (
        P("lead", "space", None, None),
        P("lead"),
        P(),
        P(),
        P(),
        P(),
        P("lead", "space", None, None),
    )
    out_specs = (P("lead", "space", None, None), P(), P(), P(), P())
    return jax.shard_map(
        per_device, mesh=mesh, in_specs=in_specs, out_specs=out_specs, check_vma=False
    )
```

```python
import functools
import math

import jax
import jax.numpy as jnp
from jax import lax
from jax.experimental import pallas as pl
from jax.experimental.pallas import tpu as pltpu
from jax.sharding import PartitionSpec as P

HDIM = 32
GRID = 8
EPSILON = 1e-05
ROWS = 4
COLS = 256
D = 512
PEERS = 8
CHUNK = 32
MESH = pl.DeviceIdType.MESH
F32 = jnp.float32
BF16 = jnp.bfloat16
VMEM_LIMIT = 61 * 1024 * 1024


def remote(src, dst, send, recv, device):
    return pltpu.make_async_remote_copy(
        src_ref=src, dst_ref=dst, send_sem=send, recv_sem=recv, device_id=device, device_id_type=MESH
    )


def dot(a, b, ca, cb):
    return lax.dot_general(a, b, (((ca,), (cb,)), ((), ())), preferred_element_type=F32)


def send_order():
    p = lax.broadcasted_iota(jnp.int32, (COLS, COLS), 0)
    col = lax.broadcasted_iota(jnp.int32, (COLS, COLS), 1)
    return jnp.where((p & 7) * 32 + (p >> 5) * 4 + ((p >> 3) & 3) == col, 1.0, 0.0).astype(BF16)


def field_order():
    p = lax.broadcasted_iota(jnp.int32, (COLS, COLS), 1)
    col = lax.broadcasted_iota(jnp.int32, (COLS, COLS), 0)
    return jnp.where((p & 7) * 32 + (p >> 5) * 4 + ((p >> 3) & 3) == col, 1.0, 0.0).astype(BF16)


def group_order():
    g = lax.broadcasted_iota(jnp.int32, (COLS, COLS), 0)
    p = lax.broadcasted_iota(jnp.int32, (COLS, COLS), 1)
    return jnp.where(((g >> 3) & 7) * 32 + (g >> 6) * 8 + (g & 7) == p, 1.0, 0.0).astype(BF16)


def attention_row(x, c, wqkv, wout, xg, cg, qkv, da, att, dp, perm, i):
    scale = 1.0 / math.sqrt(HDIM)
    c2 = scale * math.log2(math.e)
    base = pl.multiple_of(i * COLS, COLS)
    here = pl.ds(base, COLS)
    gx = dot(perm[...], x, 1, 0).astype(BF16)
    gc = dot(perm[...], c, 1, 0).astype(BF16)
    xg[here, :] = gx
    cg[here, :] = gc
    for n in range(3):
        qkv[:, n * D : (n + 1) * D] = dot(gx, wqkv[:, n * D : (n + 1) * D], 1, 0).astype(BF16)
    da[...] = dot(gc, wout[...], 1, 1).astype(BF16)
    lane = lax.broadcasted_iota(jnp.int32, (1, 128), 1) // HDIM
    masks16 = [jnp.where(lane == h, 1.0, 0.0).astype(BF16) for h in range(4)]
    lanes = lax.broadcasted_iota(jnp.int32, (64, 128), 1) // HDIM
    picks = [lanes == h for h in range(3)]

    def spread(t):
        return jnp.concatenate([t * m for m in masks16], axis=0)

    def gather(t):
        total = jnp.where(picks[2], t[128:192], t[192:256])
        total = jnp.where(picks[1], t[64:128], total)
        return jnp.where(picks[0], t[0:64], total)

    def group(g, carry):
        rows = pl.ds(pl.multiple_of(g * 64, 64), 64)
        out = pl.ds(pl.multiple_of(base + g * 64, 64), 64)
        at = [(t * 128, t * 128 + 128) for t in range(4)]
        qs = [spread(qkv[rows, lo:hi]) for lo, hi in at]
        k = [qkv[rows, D + lo : D + hi] for lo, hi in at]
        v = [qkv[rows, 2 * D + lo : 2 * D + hi] for lo, hi in at]
        ds_ = [spread(da[rows, lo:hi]) for lo, hi in at]
        s = [dot(a, b, 1, 1) for a, b in zip(k, qs)]
        dpr = [dot(a, b, 1, 1) for a, b in zip(v, ds_)]
        m = [jnp.max(a, axis=0, keepdims=True) * c2 for a in s]
        e = [jnp.exp2(a * c2 - b) for a, b in zip(s, m)]
        p = [a * (1.0 / jnp.sum(a, axis=0, keepdims=True)) for a in e]
        p16 = [a.astype(BF16) for a in p]
        inner = [jnp.sum(a * b, axis=0, keepdims=True) for a, b in zip(p, dpr)]
        dsc = [(a * (b - c)).astype(BF16) for a, b, c in zip(p, dpr, inner)]
        o1 = [dot(a, b, 0, 0) for a, b in zip(p16, v)]
        o2 = [dot(a, b, 1, 0) for a, b in zip(p16, ds_)]
        o3 = [dot(a, b, 0, 0) for a, b in zip(dsc, k)]
        o4 = [dot(a, b, 1, 0) for a, b in zip(dsc, qs)]
        for n, (lo, hi) in enumerate(at):
            att[out, lo:hi] = gather(o1[n]).astype(BF16)
            dp[out, 2 * D + lo : 2 * D + hi] = o2[n].astype(BF16)
            dp[out, lo:hi] = (gather(o3[n]) * scale).astype(BF16)
            dp[out, D + lo : D + hi] = (o4[n] * scale).astype(BF16)
        return carry

    lax.fori_loop(0, 4, group, 0)


def normed_back(dp, wqkv, i):
    here = pl.ds(pl.multiple_of(i * COLS, COLS), COLS)
    dnf = dot(dp[here, :], wqkv[...], 1, 1)
    blocks = [dnf[g * 64 + m * 8 : g * 64 + m * 8 + 8] for m in range(8) for g in range(4)]
    return jnp.concatenate(blocks, axis=0).astype(BF16).reshape(PEERS, CHUNK, D)


def grads_of(xg, cg, att, dp, here, half, n):
    if n < 3:
        return dot(xg[here, half], dp[here, n * D : (n + 1) * D], 0, 0)
    return dot(att[here, half], cg[here, :], 0, 0)


def add_grads(xg, cg, att, dp, acc, i):
    here = pl.ds(pl.multiple_of(i * COLS, COLS), COLS)
    for h in range(2):
        for n in range(4):
            half = slice(h * 256, h * 256 + 256)
            acc[h, :, n * D : (n + 1) * D] += grads_of(xg, cg, att, dp, here, half, n)


PARTS = ((0, 640, "xyz"), (640, 640, "yzx"), (1280, 768, "zxy"))
NP = len(PARTS)
WIDE = 768


def section_kernel(
    latent_any, cot_any, ck, lead_index, cond_any, wqkv_any, wout_any,
    gx_any, total_any, small,
    gx, total, latent, cot, wqkv, wout, cond, mod, halo, xp, dpad, nf, inv, nrm, fperm, gperm, bperm,
    xs, cs, xr, cr, xg, cg, qkv, da, att, dp, dn, dr, dnf, hsend, hrecv,
    acc, grads, r0, a0, r1, a1, r2, ex, ksum, tsum, sm, s1, s2, s3, s4,
    lsem, hsem, xsem, csem, dsem, bsem, wsem, rsem, gsem, ssem, osem,
):
    lead = lax.axis_index("lead")
    space = lax.axis_index("space")
    a, q = space // 4, lax.rem(space, 4)
    core, x_lo = lax.rem(lead, 2), lead // 2
    z, y, x_hi = space // 8, lax.rem(space // 2, 4), lax.rem(space, 2)
    x = x_hi * 2 + x_lo
    coord = {"x": x, "y": y, "z": z}

    def at_axis(axis, j):
        if axis == "x":
            return ((lax.rem(j, 2) * 2 + core), space - x_hi + j // 2)
        if axis == "y":
            return (lead, space + (j - y) * 2)
        return (lead, space + (j - z) * 8)

    def ahead(axis, d):
        return lax.rem(coord[axis] + d, 4)

    def behind(axis, d):
        return lax.rem(coord[axis] + 4 - d, 4)

    twin = (lead + 1 - 2 * core, space)
    has_low, has_high = space > 0, space < 31

    loads = [
        pltpu.make_async_copy(src, dst, lsem.at[n])
        for n, (src, dst) in enumerate(
            (
                (cot_any.at[1], cot.at[1]),
                (latent_any.at[0:2], latent.at[0:2]),
                (latent_any.at[2:4], latent.at[2:4]),
                (cond_any, cond),
                (cot_any.at[2:4], cot.at[2:4]),
                (cot_any.at[0], cot.at[0]),
                (wqkv_any, wqkv),
                (wout_any, wout),
            )
        )
    ]
    for load in loads:
        load.start()

    @pl.when(space == 0)
    def _():
        halo[0] = jnp.zeros((COLS, D), BF16)
        hrecv[0] = jnp.zeros((COLS, D), BF16)

    @pl.when(space == 31)
    def _():
        halo[1] = jnp.zeros((COLS, D), BF16)
        hrecv[1] = jnp.zeros((COLS, D), BF16)

    barrier = pltpu.get_barrier_semaphore()

    def greet(device):
        pl.semaphore_signal(barrier, inc=1, device_id=device, device_id_type=MESH)

    def greet_peer(d, c):
        greet((lead, 4 * lax.rem(a + d, PEERS) + q))
        return c

    lax.fori_loop(1, PEERS, greet_peer, 0)
    for axis in "xyz":
        for d in range(1, 4):
            greet(at_axis(axis, ahead(axis, d)))
    greet(twin)

    @pl.when(has_low)
    def _():
        greet((lead, space - 1))

    @pl.when(has_high)
    def _():
        greet((lead, space + 1))

    fperm[...] = send_order()
    pl.semaphore_wait(barrier, 17 + jnp.where(has_low, 1, 0) + jnp.where(has_high, 1, 0))

    def edge(src, dst, piece, sem, up):
        cells = slice(piece * 128, piece * 128 + 128)
        n = 2 * piece + (0 if up else 4)
        device = (lead, space - 1) if up else (lead, space + 1)
        return remote(src.at[cells], dst.at[1 if up else 0, cells], sem.at[n], sem.at[n + 1], device)

    def edge_start(src, dst, piece, sem, up):
        @pl.when(has_low if up else has_high)
        def _():
            edge(src, dst, piece, sem, up).start()

    def edge_wait(first, last, dst, sem):
        for piece in range(2):

            @pl.when(has_low)
            def _():
                edge(first, dst, piece, sem, True).wait_send()
                edge(last, dst, piece, sem, False).wait_recv()

            @pl.when(has_high)
            def _():
                edge(last, dst, piece, sem, False).wait_send()
                edge(first, dst, piece, sem, True).wait_recv()

    for piece in range(2):
        edge_start(latent_any.at[0], halo, piece, hsem, True)
        edge_start(latent_any.at[3], halo, piece, hsem, False)

    def send(bufs, out, sem, r):
        def one(d, c):
            t = lax.rem(a + d, PEERS)
            remote(bufs.at[r, t], out.at[r, a], sem.at[0, r, d], sem.at[1, r, d], (lead, 4 * t + q)).start()
            return c

        lax.fori_loop(1, PEERS, one, 0)
        pltpu.make_async_copy(bufs.at[r, a], out.at[r, a], sem.at[0, r, 0]).start()

    def finish(bufs, out, sem, r):
        def one(d, c):
            t = lax.rem(a + d, PEERS)
            f = lax.rem(a + PEERS - d, PEERS)
            remote(bufs.at[r, t], out.at[r, f], sem.at[0, r, d], sem.at[1, r, d], (lead, 4 * t + q)).wait()
            return c

        lax.fori_loop(1, PEERS, one, 0)
        pltpu.make_async_copy(bufs.at[r, a], out.at[r, a], sem.at[0, r, 0]).wait()

    def cot_row(r):
        cs[r] = dot(fperm[...], cot[r], 1, 0).astype(BF16).reshape(PEERS, CHUNK, D)
        send(cs, cr, csem, r)

    def norm_row(r):
        def chunk(c, carry):
            at = pl.multiple_of(c * CHUNK, CHUNK)
            w = [xp[r + m, pl.ds(at, CHUNK + 16), :] for m in range(3)]
            k = [ck[m // 3, m % 3 : m % 3 + 1, :] for m in range(9)]
            t = [k[j] * w[0] + k[3 + j] * w[1] + k[6 + j] * w[2] for j in range(3)]
            res = w[1][8 : CHUNK + 8] + (
                t[0][7 : CHUNK + 7] + t[1][8 : CHUNK + 8] + t[2][9 : CHUNK + 9]
            )
            cen = res - jnp.mean(res, axis=-1, keepdims=True)
            iv = lax.rsqrt(jnp.mean(cen * cen, axis=-1, keepdims=True) + EPSILON)
            n = cen * iv
            nf[r, pl.ds(at, CHUNK), :] = n
            inv[r, pl.ds(at, CHUNK), :] = jnp.broadcast_to(iv, (CHUNK, 128))
            nrm[pl.ds(at, CHUNK), :] = (n * (1.0 + mod[0:1, :]) + mod[1:2, :]).astype(BF16)
            return carry

        lax.fori_loop(0, COLS // CHUNK, chunk, 0)
        xs[r] = dot(fperm[...], nrm[...], 1, 0).astype(BF16).reshape(PEERS, CHUNK, D)

    def fold(t):
        total = t[0:8]
        for n in range(8, CHUNK, 8):
            total = total + t[n : n + 8]
        return total

    def back_row(r):
        finish(dn, dr, dsem, r)
        dnf[...] = dot(bperm[...], dr[r].reshape(COLS, D), 1, 0)

        def chunk(c, carry):
            at = pl.multiple_of(c * CHUNK, CHUNK)
            here = pl.ds(at, CHUNK)
            dv = dnf[here, :]
            n = nf[r, here, :]
            iv = inv[r, here, 0:1]
            tsum[0] += fold(dv * n)
            tsum[1] += fold(dv)
            g = dv * (1.0 + mod[0:1, :])
            m1 = jnp.mean(g, axis=-1, keepdims=True)
            m2 = jnp.mean(g * n, axis=-1, keepdims=True)
            res = cot[r, here, :].astype(F32) + iv * (g - m1 - n * m2)
            dpad[r + 1, pl.ds(at + 8, CHUNK), :] = res
            return carry

        lax.fori_loop(0, COLS // CHUNK, chunk, 0)

    def kernel_rows(first, last):
        def chunk(i, carry):
            r = i // (COLS // CHUNK)
            at = pl.multiple_of(lax.rem(i, COLS // CHUNK) * CHUNK, CHUNK)
            w = dpad[r + 1, pl.ds(at, CHUNK + 16), :]
            dj = [w[9 - j : 9 - j + CHUNK] for j in range(3)]
            for m in range(3):
                xw = xp[r + m, pl.ds(at + 8, CHUNK), :]
                for j in range(3):
                    ksum[3 * m + j] += fold(xw * dj[j])
            return carry

        lax.fori_loop(first * (COLS // CHUNK), last * (COLS // CHUNK), chunk, 0)

    def out_row(r):
        def chunk(c, carry):
            at = pl.multiple_of(c * CHUNK, CHUNK)
            w = [dpad[r + m, pl.ds(at, CHUNK + 16), :] for m in range(3)]
            k = [ck[m // 3, m % 3 : m % 3 + 1, :] for m in range(9)]
            t = [k[8 - j] * w[0] + k[5 - j] * w[1] + k[2 - j] * w[2] for j in range(3)]
            res = w[1][8 : CHUNK + 8] + (
                t[0][7 : CHUNK + 7] + t[1][8 : CHUNK + 8] + t[2][9 : CHUNK + 9]
            )
            gx[r, pl.ds(at, CHUNK), :] = res.astype(BF16)
            return carry

        lax.fori_loop(0, COLS // CHUNK, chunk, 0)
        keep_row(r).start()

    def span(part):
        first, width, _ = PARTS[part]
        return slice(first, first + width)

    def swap(part):
        cols = span(part)
        return remote(
            grads.at[:, cols], r0.at[:, cols], bsem.at[0, part], bsem.at[1, part], twin
        )

    def swap_end(part):
        cols = span(part)
        swap(part).wait()

        def add(c, carry):
            rows = pl.ds(pl.multiple_of(c * 32, 32), 32)
            a0[rows, cols] = (acc[core, rows, cols] + r0[rows, cols].astype(F32)).astype(BF16)
            return carry

        lax.fori_loop(0, 8, add, 0)

    def stage(k, part, waits):
        first, width, axes = PARTS[part]
        axis = axes[k]
        for d in range(1, 4):
            j = ahead(axis, d)
            if k == 0:
                src = a0.at[pl.ds(pl.multiple_of(j * 64, 64), 64), span(part)]
                dst = r1.at[part, d - 1, :, 0:width]
            elif k == 1:
                src = a1.at[part, pl.ds(pl.multiple_of(j * 16, 16), 16), 0:width]
                dst = r2.at[part, d - 1, :, 0:width]
            else:
                src = ex.at[part, coord[axis], :, 0:width]
                dst = ex.at[part, behind(axis, d) if waits else coord[axis], :, 0:width]
            cp = remote(src, dst, rsem.at[0, k, part, d], rsem.at[1, k, part, d], at_axis(axis, j))
            if waits:
                cp.wait()
            else:
                cp.start()

    def stage_start(k):
        for part in range(NP):
            stage(k, part, False)

    def stage_end(k, part):
        first, width, axes = PARTS[part]
        stage(k, part, True)
        m = coord[axes[k]]
        if k == 0:
            t = a0[pl.ds(pl.multiple_of(m * 64, 64), 64), span(part)].astype(F32)
            for d in range(3):
                t = t + r1[part, d, :, 0:width].astype(F32)
            a1[part, :, 0:width] = t.astype(BF16)
        elif k == 1:
            t = a1[part, pl.ds(pl.multiple_of(m * 16, 16), 16), 0:width].astype(F32)
            for d in range(3):
                t = t + r2[part, d, :, 0:width].astype(F32)
            ex[part, coord[axes[2]], :, 0:width] = t.astype(BF16)
        else:
            t = ex[part, 0, :, 0:width].astype(F32)
            for d in range(1, 4):
                t = t + ex[part, d, :, 0:width].astype(F32)
            rows = pl.multiple_of(coord[axes[0]] * 64 + coord[axes[1]] * 16, 16)
            total[pl.ds(rows, 16), span(part)] = t.astype(BF16)

    def block(k, part, values):
        if k == 0:
            return total.at[pl.ds(pl.multiple_of(values[0] * 64, 64), 64), span(part)]
        return total.at[pl.ds(pl.multiple_of(values[0] * 64 + values[1] * 16, 16), 16), span(part)]

    def gather(k, part, waits):
        axes = PARTS[part][2]
        mine = [coord[ax] for ax in axes]
        for d in range(1, 4):
            theirs = list(mine)
            theirs[k] = behind(axes[k], d)
            src = block(k, part, mine)
            dst = block(k, part, theirs) if waits else src
            cp = remote(src, dst, gsem.at[0, k, part, d], gsem.at[1, k, part, d], at_axis(axes[k], ahead(axes[k], d)))
            if waits:
                cp.wait()
            else:
                cp.start()

    def keep(part):
        return pltpu.make_async_copy(
            total.at[:, span(part)], total_any.at[core, :, span(part)], osem.at[part]
        )

    def twin_gather(part, waits):
        keep(part).wait() if waits else keep(part).start()
        dst = total_any.at[(1 - core) if waits else core, :, span(part)]
        cp = remote(total.at[:, span(part)], dst, bsem.at[0, NP + part], bsem.at[1, NP + part], twin)
        if waits:
            cp.wait()
        else:
            cp.start()

    def keep_row(r):
        return pltpu.make_async_copy(gx.at[r], gx_any.at[r], osem.at[NP + r])

    def small_stage(slots, axis, k, waits):
        m = coord[axis]
        for d in range(1, 4):
            dst = slots.at[behind(axis, d)] if waits else slots.at[m]
            cp = remote(slots.at[m], dst, ssem.at[0, k, d], ssem.at[1, k, d], at_axis(axis, ahead(axis, d)))
            if waits:
                cp.wait()
            else:
                cp.start()

    def small_twin(dst):
        return remote(s4.at[core], s4.at[dst], ssem.at[0, 3, 0], ssem.at[1, 3, 0], twin)

    def widen(r, c):
        xp[r + 1, 8 : COLS + 8, :] = latent[r].astype(F32)
        return c

    loads[0].wait()
    cot_row(1)
    xp[:, 0:8, :] = jnp.zeros((ROWS + 2, 8, D), F32)
    xp[:, COLS + 8 : COLS + 16, :] = jnp.zeros((ROWS + 2, 8, D), F32)
    loads[1].wait()
    loads[2].wait()
    lax.fori_loop(0, ROWS, widen, 0)
    loads[3].wait()
    mod[...] = cond[lead_index[0]]
    loads[4].wait()

    def inner_row(i, c):
        norm_row(1 + i)
        send(xs, xr, xsem, 1 + i)

        @pl.when(i == 0)
        def _():
            cot_row(2)

        return c

    lax.fori_loop(0, 2, inner_row, 0)
    loads[5].wait()
    cot_row(0)
    cot_row(3)
    gperm[...] = group_order()
    bperm[...] = field_order()
    dpad[:, 0:8, :] = jnp.zeros((ROWS + 2, 8, D), F32)
    dpad[:, COLS + 8 : COLS + 16, :] = jnp.zeros((ROWS + 2, 8, D), F32)
    ksum[...] = jnp.zeros((9, 8, D), F32)
    tsum[...] = jnp.zeros((2, 8, D), F32)
    acc[...] = jnp.zeros(acc.shape, F32)
    loads[6].wait()
    loads[7].wait()

    def edge_row(i, c):
        norm_row(3 * i)
        send(xs, xr, xsem, 3 * i)
        return c

    def step(i, c):
        r = jnp.where(i < 2, i + 1, (i - 2) * 3)

        finish(cs, cr, csem, r)
        finish(xs, xr, xsem, r)
        attention_row(
            xr[r].reshape(COLS, D), cr[r].reshape(COLS, D), wqkv, wout, xg, cg, qkv, da, att, dp, gperm, i
        )

        @pl.when(i == 0)
        def _():
            edge_wait(latent_any.at[0], latent_any.at[3], halo, hsem)
            xp[0, 8 : COLS + 8, :] = halo[0].astype(F32)
            xp[ROWS + 1, 8 : COLS + 8, :] = halo[1].astype(F32)
            lax.fori_loop(0, 2, edge_row, 0)

        @pl.when(i < 3)
        def _():
            dn[r] = normed_back(dp, wqkv, i)
            send(dn, dr, dsem, r)

        @pl.when(i < 2)
        def _():
            add_grads(xg, cg, att, dp, acc, i)

        return c

    lax.fori_loop(0, ROWS, step, 0)
    late = slice(2 * COLS, 4 * COLS)
    theirs = pl.ds(pl.multiple_of((1 - core) * 256, 256), 256)
    ours = pl.ds(pl.multiple_of(core * 256, 256), 256)
    for n in range(4):
        cols = slice(n * D, (n + 1) * D)
        grads[:, cols] = (acc[1 - core, :, cols] + grads_of(xg, cg, att, dp, late, theirs, n)).astype(BF16)
        if n > 0:
            swap(n - 1).start()
    dn[3] = normed_back(dp, wqkv, 3)
    send(dn, dr, dsem, 3)
    for n in range(4):
        acc[core, :, n * D : (n + 1) * D] += grads_of(xg, cg, att, dp, late, ours, n)
    back_row(0)
    hsend[0] = dpad[1, 8 : COLS + 8, :].astype(BF16)
    for part in range(NP):
        swap_end(part)
        stage(0, part, False)
    back_row(1)
    back_row(2)
    kernel_rows(0, 3)
    for part in range(NP):
        stage_end(0, part)
        stage(1, part, False)
    back_row(3)
    hsend[1] = dpad[4, 8 : COLS + 8, :].astype(BF16)
    kernel_rows(3, 4)
    for n in range(9):
        sm[n : n + 1, :] = jnp.sum(ksum[n], axis=0, keepdims=True)
    for n in range(2):
        sm[9 + n : 10 + n, :] = jnp.sum(tsum[n], axis=0, keepdims=True)
    sm[11:12, :] = jnp.full((1, D), lead_index[0].astype(F32) * (1.0 / 32.0))
    sm[12:16, :] = jnp.zeros((4, D), F32)
    s1[z] = sm[...]
    small_stage(s1, "z", 0, False)
    for part in range(NP):
        stage_end(1, part)
        stage(2, part, False)
    for piece in range(2):
        edge_start(hsend.at[0], hrecv, piece, wsem, True)
    out_row(1)
    out_row(2)
    small_stage(s1, "z", 0, True)
    s2[y] = s1[0] + s1[1] + s1[2] + s1[3]
    small_stage(s2, "y", 1, False)
    for part in range(NP):
        stage_end(2, part)
        gather(1, part, False)
    for piece in range(2):
        edge_start(hsend.at[1], hrecv, piece, wsem, False)
    small_stage(s2, "y", 1, True)
    s3[x] = s2[0] + s2[1] + s2[2] + s2[3]
    small_stage(s3, "x", 2, False)
    for part in range(NP):
        gather(1, part, True)
        gather(0, part, False)
    edge_wait(hsend.at[0], hsend.at[1], hrecv, wsem)
    dpad[0, 8 : COLS + 8, :] = hrecv[0].astype(F32)
    dpad[ROWS + 1, 8 : COLS + 8, :] = hrecv[1].astype(F32)
    out_row(0)
    out_row(3)
    small_stage(s3, "x", 2, True)
    s4[core, 0] = s3[0] + s3[2]
    s4[core, 1] = s3[1] + s3[3]
    small_twin(core).start()
    for part in range(NP):
        gather(0, part, True)
        twin_gather(part, False)
    small_twin(1 - core).wait()
    small[...] = s4[...]
    for r in range(ROWS):
        keep_row(r).wait()
    for part in range(NP):
        twin_gather(part, True)


STEPS = 2


def finish_kernel(
    norm_scale, table_rows, total, small, gx, grad_qkv, grad_out, grad_kernel, grad_table, grad_x
):
    step = pl.program_id(0)
    grad_x[...] = gx[...]
    whole = total[0].astype(F32) * norm_scale
    grad_qkv[...] = whole[:, : 3 * D]
    grad_out[...] = whole[:, 3 * D :]
    for n in range(9):
        row = small[0, n : n + 1, :]
        for m in range(1, 4):
            row = row + small[m, n : n + 1, :]
        grad_kernel[n // 3, n % 3 : n % 3 + 1, :] = row * norm_scale
    grad_table[...] = jnp.zeros(grad_table.shape, F32)
    for m in range(4):
        index = (jnp.max(small[m, 11:12, 0:128]) + 0.5).astype(jnp.int32) - step * table_rows

        @pl.when((index >= 0) & (index < table_rows))
        def _():
            grad_table[index] = grad_table[index] + small[m, 9:11, :] * norm_scale


def vmem(count):
    return [pl.BlockSpec(memory_space=pltpu.VMEM)] * count


def per_device(latent, lead_index, conv_kernel, cond_table, w_qkv, w_out, cotangent):
    leads = cond_table.shape[0]
    norm_scale = 1.0 / math.sqrt(4 * 128 * 256)
    shape = jax.ShapeDtypeStruct
    far = pl.BlockSpec(memory_space=pl.ANY)
    near = pl.BlockSpec(memory_space=pltpu.VMEM)
    dma = pltpu.SemaphoreType.DMA
    f32 = lambda *dims: pltpu.VMEM(dims, F32)
    bf16 = lambda *dims: pltpu.VMEM(dims, BF16)
    blocks = (ROWS, PEERS, CHUNK, D)

    grad_x, total, small = pl.pallas_call(
        section_kernel,
        out_shape=[
            shape((ROWS, COLS, D), BF16),
            shape((2, 256, 4 * D), BF16),
            shape((2, 2, 16, D), F32),
        ],
        in_specs=[far, far, near, pl.BlockSpec(memory_space=pltpu.SMEM), far, far, far],
        out_specs=[far, far, near],
        scratch_shapes=[
            bf16(ROWS, COLS, D),
            bf16(256, 4 * D),
            bf16(ROWS, COLS, D),
            bf16(ROWS, COLS, D),
            bf16(D, 3 * D),
            bf16(D, D),
            f32(leads, 2, D),
            f32(2, D),
            bf16(2, COLS, D),
            f32(ROWS + 2, COLS + 16, D),
            f32(ROWS + 2, COLS + 16, D),
            f32(ROWS, COLS, D),
            f32(ROWS, COLS, 128),
            bf16(COLS, D),
            bf16(COLS, COLS),
            bf16(COLS, COLS),
            bf16(COLS, COLS),
            bf16(*blocks),
            bf16(*blocks),
            bf16(*blocks),
            bf16(*blocks),
            bf16(ROWS * COLS, D),
            bf16(ROWS * COLS, D),
            bf16(COLS, 3 * D),
            bf16(COLS, D),
            bf16(ROWS * COLS, D),
            bf16(ROWS * COLS, 3 * D),
            bf16(*blocks),
            bf16(*blocks),
            f32(COLS, D),
            bf16(2, COLS, D),
            bf16(2, COLS, D),
            f32(2, 256, 4 * D),
            bf16(256, 4 * D),
            bf16(256, 4 * D),
            bf16(256, 4 * D),
            bf16(NP, 3, 64, WIDE),
            bf16(NP, 64, WIDE),
            bf16(NP, 3, 16, WIDE),
            bf16(NP, 4, 16, WIDE),
            f32(9, 8, D),
            f32(2, 8, D),
            f32(16, D),
            f32(4, 16, D),
            f32(4, 16, D),
            f32(4, 16, D),
            f32(2, 2, 16, D),
            dma((8,)),
            dma((8,)),
            dma((2, ROWS, PEERS)),
            dma((2, ROWS, PEERS)),
            dma((2, ROWS, PEERS)),
            dma((2, 2 * NP)),
            dma((8,)),
            dma((2, 3, NP, 4)),
            dma((2, 2, NP, 4)),
            dma((2, 4, 4)),
            dma((NP + ROWS,)),
        ],
        compiler_params=pltpu.CompilerParams(
            collective_id=1, has_side_effects=True, vmem_limit_bytes=VMEM_LIMIT
        ),
        name="section",
    )(latent[0], cotangent[0], conv_kernel, lead_index, cond_table, w_qkv, w_out)

    table_rows = -(-leads // STEPS)
    grad_qkv, grad_out, grad_kernel, grad_table, grad_x = pl.pallas_call(
        functools.partial(finish_kernel, norm_scale, table_rows),
        grid=(STEPS,),
        out_shape=[
            shape((D, 3 * D), F32),
            shape((D, D), F32),
            shape((3, 3, D), F32),
            shape((leads, 2, D), F32),
            shape((ROWS, COLS, D), BF16),
        ],
        in_specs=[
            pl.BlockSpec((1, 512 // STEPS, 4 * D), lambda i: (i, 0, 0)),
            pl.BlockSpec((4, 16, D), lambda i: (0, 0, 0)),
            pl.BlockSpec((ROWS // STEPS, COLS, D), lambda i: (i, 0, 0)),
        ],
        out_specs=[
            pl.BlockSpec((512 // STEPS, 3 * D), lambda i: (i, 0)),
            pl.BlockSpec((512 // STEPS, D), lambda i: (i, 0)),
            pl.BlockSpec((3, 3, D), lambda i: (0, 0, 0)),
            pl.BlockSpec((table_rows, 2, D), lambda i: (i, 0, 0)),
            pl.BlockSpec((ROWS // STEPS, COLS, D), lambda i: (i, 0, 0)),
        ],
        compiler_params=pltpu.CompilerParams(vmem_limit_bytes=VMEM_LIMIT),
        name="finish",
    )(total, small.reshape(4, 16, D), grad_x)
    return (grad_x[None], grad_qkv, grad_out, grad_kernel, grad_table)


def solution(mesh):
    in_specs = (
        P("lead", "space", None, None),
        P("lead"),
        P(),
        P(),
        P(),
        P(),
        P("lead", "space", None, None),
    )
    out_specs = (P("lead", "space", None, None), P(), P(), P(), P())
    return jax.shard_map(
        per_device, mesh=mesh, in_specs=in_specs, out_specs=out_specs, check_vma=False
    )
```
